32 devices in a mesh: dp: 16 (over z, x, core), mp: 2 (over y).
Axes of the slice: x: 2, y: 2, z: 4, core: 2. Of those that a mesh axis runs over, the one named last changes fastest.
Arguments:
- resp_q: bfloat16 [16, 128, 8192], P('dp', None, 'mp'), may hold values from -12 to 12, as said below
- resp_kv: bfloat16 [2, 16, 128, 1024], P(None, 'dp', None, 'mp'), may hold values from -4 to 4
- d_out: bfloat16 [16, 128, 8192], P('dp', None, 'mp'), may hold values from -6 to 6
- lengths: int32 [16], P('dp'), may hold values from 1 to 128, 1536 in all
- fork: int32 [16], replicated, may hold values from 0 to 31
- page_table: int32 [32, 8], replicated, may hold values from 0 to 255, as said below
- pool_pages: bfloat16 [256, 2, 16, 1024], P(('dp', 'mp')), may hold values from -4 to 4
- pool_scales: bfloat16 [256, 2, 8], P(('dp', 'mp')), may hold values from 0.29882812 to 3
Outputs:
- d_query: bfloat16 [16, 128, 8192], P('dp', None, 'mp')
- d_resp_kv: bfloat16 [2, 16, 128, 1024], P(None, 'dp', None, 'mp')
- d_pool: float32 [256, 2, 16, 1024], P(('dp', 'mp'))
The draws below stay inside these ranges and needn't reach their ends.
Inputs may be any that keep to these rules, and one draw needn't show every extreme that they name: `page_table`: every pool page is named exactly once. Pool page g lies on dp index g // 16, and the 8 pages of one prompt lie on 8 different dp indices. `resp_q`: query entries. On some rows, some query heads may be a multiple between 1.5 and 3 of a key of the same response, so that scores can reach several hundred.
All inputs are finite; a program needn't handle non-finite values. No bound on the sum of `lengths` on one device may be relied on, other than what follows from the above.
Results may differ from the reference program's by a relative error of at most 0.012.
Values may be sent and summed in bfloat16 or wider, within the bound.
A program may use at most 64 MiB of HBM per device.

```python
import math
import jax
import jax.numpy as jnp
import numpy as np
from jax import lax

HQ = 64
KVH = 8
DH = 128
GROUP = 8
PAGE = 16
RLEN = 128
PAGES_DEV = 8
PAGES = 8
RESPONSES = 16
PROMPTS = 32
POOL = 256
N_DP = 16
N_MP = 2


def shared_keys(key, strength):
    base_keys = jnp.clip(jax.random.normal(key, (RESPONSES, RLEN, KVH * DH), jnp.float32), -4.0, 4.0)
    step_pos = jnp.arange(RLEN)
    marked = (step_pos % 29 == 7).astype(jnp.float32)[None, :, None] * strength
    following = jnp.roll(marked, -1, axis=1)
    signs = jnp.where(base_keys >= 0.0, 1.0, -1.0)
    big_keys = 4.0 * signs
    lowered = (jnp.arange(KVH * DH) % DH < max(DH // 16, 1)).astype(jnp.float32)[None, None, :]
    near_keys = big_keys * (1.0 - lowered) + 3.75 * signs * lowered
    following_near = jnp.roll(near_keys, -1, axis=1)
    mixed_keys = base_keys * (1.0 - marked - following) + following * following_near
    return (mixed_keys, marked)


def draw_resp_q(key, part):
    strength = 0.0
    mixed_keys, marked = shared_keys(key, strength)
    key = jax.random.fold_in(key, 3)
    drawn_rows = jnp.clip(jax.random.normal(key, (RESPONSES, RLEN, KVH, HQ // KVH, DH), jnp.float32), -4.0, 4.0)
    head_ids = jnp.arange(HQ).reshape(KVH, HQ // KVH)
    head_mark = (head_ids % 4 == 1).astype(jnp.float32)[None, None, :, :, None]
    chosen = marked[..., None, None] * head_mark
    result = drawn_rows * (1.0 - chosen)
    return result.reshape(RESPONSES, RLEN, HQ * DH).astype(jnp.bfloat16)


def draw_resp_kv(key, part):
    strength = 0.0
    mixed_keys, marked = shared_keys(key, strength)
    key = jax.random.fold_in(key, 5)
    values = jnp.clip(jax.random.normal(key, (RESPONSES, RLEN, KVH * DH), jnp.float32), -4.0, 4.0)
    return jnp.stack([mixed_keys, values]).astype(jnp.bfloat16)


def draw_page_table(key, part):
    key = jax.random.fold_in(key, 7)
    key_spread, key_shift, key_slot, key_order = jax.random.split(key, 4)
    per_dev = N_MP * PAGES_DEV
    spread = jax.random.permutation(key_spread, N_DP)
    shifts = jax.random.randint(key_shift, (per_dev,), 0, N_DP)
    scores = jax.random.randint(key_slot, (N_DP, per_dev), 0, 1 << 20) * per_dev + jnp.arange(per_dev)[None, :]
    slot_of = jnp.argsort(scores, axis=1)
    prompt_order = jax.random.permutation(key_order, PROMPTS)
    half_index = prompt_order // per_dev
    column = prompt_order % per_dev
    logical = jnp.arange(PAGES)
    position = (half_index[:, None] * PAGES + logical[None, :] + shifts[column][:, None]) % N_DP
    device = spread[position]
    slot_index = slot_of[device, column[:, None]]
    return (device * per_dev + slot_index).astype(jnp.int32)


def touch_ends(values, stream_key, low, top_value):
    dims = values.shape
    spot = [jax.random.randint(jax.random.fold_in(stream_key, axis), (), 0, dims[axis]) for axis in range(len(dims))]
    values = values.at[tuple(spot)].set(low)
    longest = dims.index(max(dims))
    spot[longest] = (spot[longest] + 1) % dims[longest]
    return values.at[tuple(spot)].set(top_value)


def level_of(own_key, shape, cuts, least, top_value):
    def one(dim, parts):
        heights = jax.random.uniform(jax.random.fold_in(jax.random.fold_in(own_key, 6), dim), (parts,), jnp.float32, least / len(cuts), top_value / len(cuts))
        return jnp.repeat(jnp.exp(heights), shape[dim] // parts).reshape((-1,) + (1,) * (len(shape) - dim - 1))

    level = one(*cuts[0])
    for cut in cuts[1:]:
        level = level * one(*cut)
    return level


def cumulative_ranks(number_of, slope):
    loads = [(1 << 20) // math.isqrt(grade ** slope) + 1 for grade in range(1, number_of + 1)]
    deviation = 1 + sum(loads) // (1 << 30)
    return np.cumsum(np.array([max(1, weight // deviation) for weight in loads]))


def skewed_ids(own_key, extent, number_of, lean):
    listing = cumulative_ranks(number_of, lean)
    ticket = jax.random.randint(jax.random.fold_in(own_key, 1), extent, 0, int(listing[number_of - 1]))
    rank = jnp.searchsorted(jnp.asarray(listing, jnp.int32), ticket, side="right")
    return jax.random.permutation(jax.random.fold_in(own_key, 2), number_of)[rank].astype(jnp.int32)


def length_profile(amount, total, limit, slope):
    loads = [(1 << 20) // math.isqrt(standing ** slope) + 1 for standing in range(2, amount + 1)]
    spare, holding = total - limit - (amount - 1), [1] * (amount - 1)
    while spare > 0:
        movable = [i for i in range(amount - 1) if holding[i] < limit]
        mass, budget = sum([loads[i] for i in movable]), spare
        for i in movable:
            addition = min(limit - holding[i], max(1, budget * loads[i] // mass), spare)
            holding[i] = holding[i] + addition
            spare = spare - addition
    return np.array([limit] + holding)


def uneven(own_key, count, total, limit, skew):
    if count == 2:
        one = jax.random.randint(own_key, (), max(1, total - limit), min(limit, total - 1) + 1)
        return jnp.stack([one, total - one])
    tallies = jnp.asarray(length_profile(count, total, limit, skew), jnp.int32)
    couples = (count - 1) // 2
    donor, taker = tallies[1:1 + 2 * couples:2], tallies[2:2 + 2 * couples:2]
    slack = jnp.minimum(donor - 1, limit - taker)
    moved = jax.random.randint(jax.random.fold_in(own_key, 1), (couples,), 0, 1 << 20) % (slack + 1)
    tallies = tallies.at[1:1 + 2 * couples:2].set(donor - moved).at[2:2 + 2 * couples:2].set(taker + moved)
    return tallies[jax.random.permutation(jax.random.fold_in(own_key, 2), count)]


def normal_values(key, dims, scale, limit, pieces=(), kind=jnp.bfloat16):
    values = jax.random.normal(key, dims, jnp.float32) * scale
    if len(pieces) > 0:
        values = level_of(key, dims, pieces, -0.22, 0.18) * values
    return jnp.clip(values, min=-limit, max=limit).astype(kind)


def setup_inputs(seed: int = 0) -> dict:
    arg_keys = jax.random.split(jax.random.key(seed), 9)
    resp_q = draw_resp_q(jax.random.fold_in(arg_keys[8], 71), 0)
    resp_kv = draw_resp_kv(jax.random.fold_in(arg_keys[8], 71), 0)
    d_out = normal_values(arg_keys[2], (RESPONSES, RLEN, HQ * DH), 1.0, 6.0, ((0, 16), (2, 2)))
    lengths = uneven(arg_keys[3], RESPONSES, RESPONSES * RLEN * 3 // 4, RLEN, 1).astype(jnp.int32)
    fork = touch_ends(skewed_ids(arg_keys[4], (RESPONSES,), PROMPTS, 2), jax.random.fold_in(arg_keys[4], 3), 0, PROMPTS - 1).astype(jnp.int32)
    page_table = draw_page_table(jax.random.fold_in(arg_keys[8], 71), 0)
    pool_pages = normal_values(arg_keys[6], (POOL, 2, PAGE, KVH * DH), 1.0, 4.0, ((0, 32),))
    pool_scales = jnp.clip(jnp.exp(math.log(3.0) - 2.306499 * jax.random.uniform(arg_keys[7], (POOL, 2, KVH), jnp.float32) ** level_of(arg_keys[7], (POOL, 2, KVH), ((0, 32),), -0.2, 0.2)), 0.29882812, 3.0).astype(jnp.bfloat16)
    return {"resp_q": resp_q, "resp_kv": resp_kv, "d_out": d_out, "lengths": lengths, "fork": fork, "page_table": page_table, "pool_pages": pool_pages, "pool_scales": pool_scales}


def dequantize(stored, factors):
    heads = factors.shape[-1]
    head_width = stored.shape[-1] // heads
    shaped = stored.astype(jnp.float32).reshape(stored.shape[0], 2, stored.shape[2], heads, head_width)
    scaled = shaped * factors.astype(jnp.float32).reshape(stored.shape[0], 2, 1, heads, 1)
    return scaled.astype(jnp.bfloat16).reshape(stored.shape)


def one_response(query_rows, own_kv, grad_rows, length, prompt_pages):
    prompt_len = PAGES * PAGE
    total = prompt_len + RLEN
    inv_root = 1.0 / (DH ** 0.5)
    key_all = jnp.concatenate([prompt_pages[:, 0].reshape(prompt_len, KVH * DH), own_kv[0]], 0)
    value_all = jnp.concatenate([prompt_pages[:, 1].reshape(prompt_len, KVH * DH), own_kv[1]], 0)
    key_heads = key_all.reshape(total, KVH, DH).transpose(1, 0, 2).astype(jnp.float32)
    value_heads = value_all.reshape(total, KVH, DH).transpose(1, 0, 2).astype(jnp.float32)
    row_pos = jnp.arange(RLEN)
    live = (row_pos < length)[:, None]
    grad_masked = jnp.where(live, grad_rows, jnp.zeros_like(grad_rows))
    query_heads = query_rows.reshape(RLEN, KVH, GROUP, DH).transpose(1, 2, 0, 3).astype(jnp.float32)
    grad_heads = grad_masked.reshape(RLEN, KVH, GROUP, DH).transpose(1, 2, 0, 3).astype(jnp.float32)
    scores = jnp.einsum("jgtd,jud->jgtu", query_heads, key_heads) * inv_root
    key_cols = jnp.arange(total)
    allowed = (key_cols[None, :] < prompt_len) | (key_cols[None, :] - prompt_len <= row_pos[:, None])
    scores = jnp.where(allowed, scores, -1e30)
    row_max = jnp.max(scores, axis=-1, keepdims=True)
    exp_scores = jnp.exp(scores - row_max)
    weights = exp_scores / jnp.sum(exp_scores, axis=-1, keepdims=True)
    weights_b = lax.optimization_barrier(weights.astype(jnp.bfloat16)).astype(jnp.float32)
    attn_out = jnp.einsum("jgtu,jud->jgtd", weights_b, value_heads)
    row_delta = jnp.sum(grad_heads * attn_out, axis=-1)
    grad_weights = jnp.einsum("jgtd,jud->jgtu", grad_heads, value_heads)
    grad_scores = weights * (grad_weights - row_delta[..., None])
    grad_scores = lax.optimization_barrier(grad_scores.astype(jnp.bfloat16)).astype(jnp.float32)
    grad_query = jnp.einsum("jgtu,jud->jgtd", grad_scores, key_heads) * inv_root
    grad_query = grad_query.transpose(2, 0, 1, 3).reshape(RLEN, HQ * DH).astype(jnp.bfloat16)
    grad_keys = jnp.einsum("jgtu,jgtd->jud", grad_scores, query_heads) * inv_root
    grad_values = jnp.einsum("jgtu,jgtd->jud", weights_b, grad_heads)
    own_keys = grad_keys[:, prompt_len:].transpose(1, 0, 2).reshape(RLEN, KVH * DH)
    own_values = grad_values[:, prompt_len:].transpose(1, 0, 2).reshape(RLEN, KVH * DH)
    own_grads = jnp.stack([own_keys, own_values]).astype(jnp.bfloat16)
    prompt_grad = jnp.stack([grad_keys[:, :prompt_len], grad_values[:, :prompt_len]])
    prompt_grad = prompt_grad.reshape(2, KVH, PAGES, PAGE, DH).transpose(2, 0, 3, 1, 4).reshape(PAGES, 2, PAGE, KVH * DH)
    return grad_query, own_grads, prompt_grad


def reference(resp_q, resp_kv, d_out, lengths, fork, page_table, pool_pages, pool_scales):
    def step_fn(pool_grad, block_items):
        query_rows, own_kv, grad_rows, length, prompt = block_items
        page_ids = page_table[prompt]
        prompt_pages = dequantize(pool_pages[page_ids], pool_scales[page_ids])
        grad_query, own_grads, prompt_grad = one_response(query_rows, own_kv, grad_rows, length, prompt_pages)
        pool_grad = pool_grad.at[page_ids].add(prompt_grad)
        return pool_grad, (grad_query, own_grads)

    start = jnp.zeros(pool_pages.shape, jnp.float32)
    pool_grad, (d_query, own_all) = lax.scan(step_fn, start, (resp_q, resp_kv.transpose(1, 0, 2, 3), d_out, lengths, fork))
    return d_query, own_all.transpose(1, 0, 2, 3), pool_grad
```

```python
import functools
import math

import jax
import jax.numpy as jnp
from jax import lax
from jax.experimental import pallas as pl
from jax.experimental.pallas import tpu as pltpu
from jax.sharding import PartitionSpec as P

DH = 128
MESH = pl.DeviceIdType.MESH
BF16 = jnp.bfloat16
F32 = jnp.float32
ACROSS = (((1,), (1,)), ((), ()))


def split_rows(rows):
    size = min(rows, 512)
    while rows % size:
        size //= 2
    return size, rows // size


def over_blocks(rows, body):
    size, count = split_rows(rows)
    if count == 1:
        body(0, size)
    else:

        @pl.loop(0, count)
        def _(b):
            body(pl.multiple_of(b * size, size), size)


def kernel(
    dp,
    mp,
    kv,
    group,
    slot,
    pages_ref,
    scales_ref,
    send_col,
    send_row,
    recv_col,
    recv_row,
    length_ref,
    q_hbm,
    g_hbm,
    rkv_hbm,
    dq_hbm,
    dkv_hbm,
    pool_hbm,
    q_buf,
    g_buf,
    rkv_buf,
    dq_buf,
    dkv_buf,
    pool_buf,
    pick,
    pick_t,
    take,
    take_t,
    slab,
    grouped,
    outgoing,
    arrived,
    back,
    returned,
    summed,
    part_out,
    part_in,
    in_sem,
    out_sem,
    mp_send,
    mp_recv,
    dp_send,
    dp_recv,
    rt_send,
    rt_recv,
    fm_send,
    fm_recv,
):
    my_dp = lax.axis_index("dp")
    my_mp = lax.axis_index("mp")
    store_rows = pages_ref.shape[0]
    resp_len = q_buf.shape[0]
    prompt_len = take.shape[0] // 2
    total = prompt_len + resp_len
    inv_root = 1.0 / DH**0.5
    to_exp2 = inv_root * math.log2(math.e)

    barrier = pltpu.get_barrier_semaphore()

    @pl.loop(1, dp)
    def _(k):
        pl.semaphore_signal(
            barrier, inc=1, device_id={"dp": lax.rem(my_dp + k, dp)}, device_id_type=MESH
        )

    for k in range(1, mp):
        pl.semaphore_signal(
            barrier, inc=1, device_id={"mp": lax.rem(my_mp + k, mp)}, device_id_type=MESH
        )

    loads = [
        pltpu.make_async_copy(rkv_hbm, rkv_buf, in_sem.at[0]),
        pltpu.make_async_copy(q_hbm.at[0], q_buf, in_sem.at[1]),
        pltpu.make_async_copy(g_hbm.at[0], g_buf, in_sem.at[2]),
    ]
    for load in loads:
        load.start()

    for head in range(mp * kv):
        lanes = slice(head * DH, (head + 1) * DH)
        scaled = pages_ref[:, lanes].astype(F32) * scales_ref[:, head : head + 1]
        slab[head] = scaled.astype(BF16)
    pl.semaphore_wait(barrier, dp + mp - 2)

    my_rows = pl.ds(pl.multiple_of(my_mp * store_rows, store_rows), store_rows)
    for j in range(kv):
        for k in range(1, mp):
            other = lax.rem(my_mp + k, mp)
            pltpu.make_async_remote_copy(
                src_ref=slab.at[other * kv + j],
                dst_ref=grouped.at[j, my_rows],
                send_sem=mp_send.at[j],
                recv_sem=mp_recv.at[j],
                device_id={"mp": other},
                device_id_type=MESH,
            ).start()
    for j in range(kv):
        grouped[j, my_rows] = slab[my_mp * kv + j]

    def build(out_ref, codes_ref, by_column):
        def body(start, size):
            shape = (size, out_ref.shape[1])
            if by_column:
                hit = codes_ref[pl.ds(start, size), :] == lax.broadcasted_iota(jnp.int32, shape, 1)
            else:
                hit = codes_ref[...] == lax.broadcasted_iota(jnp.int32, shape, 0) + start
            out_ref[pl.ds(start, size), :] = jnp.where(hit, 1.0, 0.0).astype(BF16)

        over_blocks(out_ref.shape[0], body)

    def select(out_ref, matrix, operand):
        def body(start, size):
            rows = pl.ds(start, size)
            out_ref[rows, :] = jnp.dot(
                matrix[rows, :], operand, preferred_element_type=F32
            ).astype(out_ref.dtype)

        over_blocks(out_ref.shape[0], body)

    build(pick, send_col, True)

    my_slot = pl.ds(pl.multiple_of(my_dp * slot, slot), slot)

    def exchange(j, source, target, send_sem, recv_sem):
        @pl.loop(1, dp)
        def _(k):
            other = lax.rem(my_dp + k, dp)
            pltpu.make_async_remote_copy(
                src_ref=source.at[j, pl.ds(pl.multiple_of(other * slot, slot), slot)],
                dst_ref=target.at[j, my_slot],
                send_sem=send_sem.at[j],
                recv_sem=recv_sem.at[j],
                device_id={"dp": other},
                device_id_type=MESH,
            ).start()

        target[j, my_slot] = source[j, my_slot]

    def wait_bytes(view, sem):
        pltpu.make_async_copy(view, view, sem).wait()

    dp_rows = pl.ds(0, (dp - 1) * slot)
    mp_rows = pl.ds(0, (mp - 1) * store_rows)
    for j in range(kv):
        if mp > 1:
            wait_bytes(grouped.at[j, mp_rows], mp_recv.at[j])
        select(outgoing.at[j], pick, grouped[j])
        exchange(j, outgoing, arrived, dp_send, dp_recv)

    build(take, recv_col, True)
    build(take_t, recv_row, False)
    build(pick_t, send_row, False)
    for load in loads:
        load.wait()

    length = length_ref[0]
    live = lax.broadcasted_iota(jnp.int32, (resp_len, DH), 0) < length
    own_shape = (resp_len, 2 * resp_len)
    causal = lax.broadcasted_iota(jnp.int32, own_shape, 0) <= lax.rem(
        lax.broadcasted_iota(jnp.int32, own_shape, 1), resp_len
    )

    for j in range(kv):
        lanes = slice(j * DH, (j + 1) * DH)
        wait_bytes(arrived.at[j, dp_rows], dp_recv.at[j])
        prompt = jnp.dot(take[...], arrived[j], preferred_element_type=F32).astype(BF16)
        keys = jnp.concatenate([prompt[:prompt_len], rkv_buf[0, 0, :, lanes]], 0)
        values = jnp.concatenate([prompt[prompt_len:], rkv_buf[1, 0, :, lanes]], 0)
        keys_t = keys.astype(F32).T.astype(BF16)
        key_grad = jnp.zeros((total, DH), F32)
        value_grad = jnp.zeros((total, DH), F32)
        for first in range(0, group, 2):
            base = (j * group + first) * DH
            heads = [slice(base, base + DH), slice(base + DH, base + 2 * DH)]
            queries = jnp.concatenate([q_buf[:, h] for h in heads], 0)
            grads = jnp.concatenate(
                [jnp.where(live, g_buf[:, h], jnp.zeros((), BF16)) for h in heads], 0
            )
            scores = lax.dot_general(keys, queries, ACROSS, preferred_element_type=F32)
            scores = jnp.concatenate(
                [scores[:prompt_len], jnp.where(causal, scores[prompt_len:], -1e30)], 0
            )
            top = jnp.max(scores, axis=0, keepdims=True)
            powers = jnp.exp2((scores - top) * to_exp2)
            weights = powers * (1.0 / jnp.sum(powers, axis=0, keepdims=True))
            weights_b = weights.astype(BF16)
            grad_weights = lax.dot_general(values, grads, ACROSS, preferred_element_type=F32)
            delta = jnp.sum(weights_b.astype(F32) * grad_weights, axis=0, keepdims=True)
            grad_scores = (weights * (grad_weights - delta)).astype(BF16)
            query_t = jnp.dot(keys_t, grad_scores, preferred_element_type=F32) * inv_root
            query_grad = query_t.T.astype(BF16)
            for i, h in enumerate(heads):
                dq_buf[:, h] = query_grad[i * resp_len : (i + 1) * resp_len]
            key_grad += jnp.dot(grad_scores, queries, preferred_element_type=F32)
            value_grad += jnp.dot(weights_b, grads, preferred_element_type=F32)
        key_grad = key_grad * inv_root
        dkv_buf[0, 0, :, lanes] = key_grad[prompt_len:].astype(BF16)
        dkv_buf[1, 0, :, lanes] = value_grad[prompt_len:].astype(BF16)
        prompt_grad = jnp.concatenate([key_grad[:prompt_len], value_grad[:prompt_len]], 0)
        select(back.at[j], take_t, prompt_grad.astype(BF16))
        exchange(j, back, returned, rt_send, rt_recv)

    stores = [
        pltpu.make_async_copy(dq_buf, dq_hbm.at[0], out_sem.at[0]),
        pltpu.make_async_copy(dkv_buf, dkv_hbm, out_sem.at[1]),
    ]
    for store in stores:
        store.start()

    def column(m, j):
        return pl.ds(pl.multiple_of((m * kv + j) * DH, DH), DH)

    for j in range(kv):
        wait_bytes(returned.at[j, dp_rows], rt_recv.at[j])
        select(summed, pick_t, returned[j])
        for k in range(1, mp):
            other = lax.rem(my_mp + k, mp)
            rows = pl.ds(pl.multiple_of(other * store_rows, store_rows), store_rows)
            part_out[other * kv + j] = summed[rows, :].astype(BF16)
            pltpu.make_async_remote_copy(
                src_ref=part_out.at[other * kv + j],
                dst_ref=part_in.at[j, my_mp],
                send_sem=fm_send.at[j],
                recv_sem=fm_recv.at[j],
                device_id={"mp": other},
                device_id_type=MESH,
            ).start()
        pool_buf[:, column(my_mp, j)] = summed[my_rows, :]
    for j in range(kv):
        if mp > 1:
            wait_bytes(part_in.at[j, pl.ds(0, mp - 1)], fm_recv.at[j])
        for k in range(1, mp):
            other = lax.rem(my_mp + k, mp)
            pool_buf[:, column(other, j)] = part_in[j, other].astype(F32)
    last = pltpu.make_async_copy(pool_buf, pool_hbm, out_sem.at[2])
    last.start()
    for j in range(kv):
        if mp > 1:
            wait_bytes(grouped.at[j, mp_rows], mp_send.at[j])
            wait_bytes(part_in.at[j, pl.ds(0, mp - 1)], fm_send.at[j])
        wait_bytes(arrived.at[j, dp_rows], dp_send.at[j])
        wait_bytes(returned.at[j, dp_rows], rt_send.at[j])
    for store in stores:
        store.wait()
    last.wait()


def per_device(resp_q, resp_kv, d_out, lengths, fork, page_table, pool_pages, pool_scales):
    dp = lax.axis_size("dp")
    mp = lax.axis_size("mp")
    my_dp = lax.axis_index("dp")
    pool_dev, _, page_rows, width = pool_pages.shape
    heads_kv = pool_scales.shape[-1]
    kv = heads_kv // mp
    pages_prompt = page_table.shape[1]
    prompt_len = pages_prompt * page_rows
    resp_len = resp_q.shape[1]
    group = resp_q.shape[2] // DH // kv
    group_pages = mp * pool_dev
    slot = 2 * page_rows
    store_rows = pool_dev * slot
    group_rows = mp * store_rows
    slots = dp * slot

    wanted = jnp.take(page_table, fork, axis=0)
    here = wanted // group_pages == my_dp
    rows = jnp.sum(jnp.where(here, wanted % group_pages + 1, 0), axis=1) - 1
    inside = jnp.arange(slot, dtype=jnp.int32)
    send_code = jnp.where(rows[:, None] >= 0, rows[:, None] * slot + inside[None, :], -1)
    sources = jnp.take(wanted, my_dp, axis=0) // group_pages
    recv_code = sources[None, :, None] * slot + inside.reshape(2, 1, page_rows)
    scales = jnp.broadcast_to(
        pool_scales.astype(F32)[:, :, None, :], (pool_dev, 2, page_rows, heads_kv)
    )

    vmem = pl.BlockSpec(memory_space=pltpu.VMEM)
    smem = pl.BlockSpec(memory_space=pltpu.SMEM)
    hbm = pl.BlockSpec(memory_space=pl.ANY)
    dma = pltpu.SemaphoreType.DMA
    total = prompt_len + resp_len
    d_query, d_kv, d_pool = pl.pallas_call(
        functools.partial(kernel, dp, mp, kv, group, slot),
        out_shape=(
            jax.ShapeDtypeStruct(resp_q.shape, BF16),
            jax.ShapeDtypeStruct(resp_kv.shape, BF16),
            jax.ShapeDtypeStruct((store_rows, width), F32),
        ),
        in_specs=[vmem] * 6 + [smem] + [hbm] * 3,
        out_specs=(hbm, hbm, hbm),
        scratch_shapes=[
            pltpu.VMEM(resp_q.shape[1:], BF16),
            pltpu.VMEM(d_out.shape[1:], BF16),
            pltpu.VMEM(resp_kv.shape, BF16),
            pltpu.VMEM(resp_q.shape[1:], BF16),
            pltpu.VMEM(resp_kv.shape, BF16),
            pltpu.VMEM((store_rows, width), F32),
            pltpu.VMEM((slots, group_rows), BF16),
            pltpu.VMEM((group_rows, slots), BF16),
            pltpu.VMEM((2 * prompt_len, slots), BF16),
            pltpu.VMEM((slots, 2 * prompt_len), BF16),
            pltpu.VMEM((heads_kv, store_rows, DH), BF16),
            pltpu.VMEM((kv, group_rows, DH), BF16),
            pltpu.VMEM((kv, slots, DH), BF16),
            pltpu.VMEM((kv, slots, DH), BF16),
            pltpu.VMEM((kv, slots, DH), BF16),
            pltpu.VMEM((kv, slots, DH), BF16),
            pltpu.VMEM((group_rows, DH), F32),
            pltpu.VMEM((heads_kv, store_rows, DH), BF16),
            pltpu.VMEM((kv, mp, store_rows, DH), BF16),
            dma((3,)),
            dma((3,)),
        ]
        + [dma((kv,))] * 8,
        compiler_params=pltpu.CompilerParams(
            collective_id=0, has_side_effects=True, vmem_limit_bytes=56 * 1024 * 1024
        ),
        cost_estimate=pl.CostEstimate(
            flops=10 * group * kv * resp_len * total * DH,
            bytes_accessed=8 * resp_q.shape[1] * resp_q.shape[2],
            transcendentals=group * kv * resp_len * total,
        ),
    )(
        pool_pages.reshape(store_rows, width),
        scales.reshape(store_rows, heads_kv),
        send_code.reshape(slots, 1),
        send_code.reshape(1, slots),
        recv_code.reshape(2 * prompt_len, 1),
        recv_code.reshape(1, 2 * prompt_len),
        lengths,
        resp_q,
        d_out,
        resp_kv,
    )
    return (d_query, d_kv, d_pool.reshape(pool_pages.shape))


def solution(mesh):
    return jax.shard_map(
        per_device,
        mesh=mesh,
        in_specs=(
            P("dp", None, "mp"),
            P(None, "dp", None, "mp"),
            P("dp", None, "mp"),
            P("dp"),
            P(),
            P(),
            P(("dp", "mp"), None, None, None),
            P(("dp", "mp"), None, None),
        ),
        out_specs=(
            P("dp", None, "mp"),
            P(None, "dp", None, "mp"),
            P(("dp", "mp"), None, None, None),
        ),
        check_vma=False,
    )
```

```python
import functools
import math

import jax
import jax.numpy as jnp
from jax import lax
from jax.experimental import pallas as pl
from jax.experimental.pallas import tpu as pltpu
from jax.sharding import PartitionSpec as P

DH = 128
WIDTH = 1
MESH = pl.DeviceIdType.MESH
BF16 = jnp.bfloat16
F32 = jnp.float32
ACROSS = (((1,), (1,)), ((), ()))


def split_rows(rows):
    size = min(rows, 512)
    while rows % size:
        size //= 2
    return size, rows // size


def over_blocks(rows, body):
    size, count = split_rows(rows)
    if count == 1:
        body(0, size)
    else:

        @pl.loop(0, count)
        def _(b):
            body(pl.multiple_of(b * size, size), size)


def partner_order(count):
    half, quarter = count // 2, count // 4
    order = []
    for i in range(quarter):
        order += [half + i, half + quarter + i, quarter + i]
    rest = [k for k in range(1, count) if k not in order]
    return [k for k in order if 0 < k < count] + rest


def ones_where(hit):
    return jnp.where(hit, 1.0, 0.0).astype(BF16)


def kernel(
    dp,
    mp,
    kv,
    group,
    width,
    scales_ref,
    fork_ref,
    table_ref,
    length_ref,
    pages_hbm,
    q_hbm,
    g_hbm,
    rkv_hbm,
    dq_hbm,
    dkv_hbm,
    pool_hbm,
    pages_ref,
    q_buf,
    g_buf,
    rkv_buf,
    dq_buf,
    dkv_buf,
    pool_buf,
    pick,
    pick_t,
    take,
    take_t,
    slab,
    grouped,
    outgoing,
    arrived,
    back,
    returned,
    summed,
    part_out,
    part_in,
    codes,
    in_sem,
    out_sem,
    mp_send,
    mp_recv,
    dp_send,
    dp_recv,
    rt_send,
    rt_recv,
    fm_send,
    fm_recv,
):
    my_dp = lax.axis_index("dp")
    my_mp = lax.axis_index("mp")
    pool_dev = scales_ref.shape[0]
    store_rows = pages_ref.shape[0]
    slot = store_rows // pool_dev
    page_rows = slot // 2
    group_pages = mp * pool_dev
    pages_prompt = table_ref.shape[0]
    resp_len = q_buf.shape[0]
    prompt_len = pages_prompt * page_rows
    total = prompt_len + resp_len
    chunks = kv // width
    span = width * DH
    inv_root = 1.0 / DH**0.5
    to_exp2 = inv_root * math.log2(math.e)

    pages_load = pltpu.make_async_copy(pages_hbm, pages_ref, in_sem.at[3])
    pages_load.start()
    barrier = pltpu.get_barrier_semaphore()

    @pl.loop(1, dp)
    def _(k):
        pl.semaphore_signal(
            barrier, inc=1, device_id={"dp": lax.rem(my_dp + k, dp)}, device_id_type=MESH
        )

    for k in range(1, mp):
        pl.semaphore_signal(
            barrier, inc=1, device_id={"mp": lax.rem(my_mp + k, mp)}, device_id_type=MESH
        )

    loads = [
        pltpu.make_async_copy(rkv_hbm, rkv_buf, in_sem.at[0]),
        pltpu.make_async_copy(q_hbm.at[0], q_buf, in_sem.at[1]),
        pltpu.make_async_copy(g_hbm.at[0], g_buf, in_sem.at[2]),
    ]
    for load in loads:
        load.start()

    factors = []
    for n in range(pool_dev):
        pair = scales_ref[n].astype(F32)
        for c in range(2):
            factors.append(jnp.broadcast_to(pair[c : c + 1, :], (page_rows, mp * kv)))
    factors = jnp.concatenate(factors, 0)
    pages_load.wait()
    for head in range(mp * kv):
        lanes = slice(head * DH, (head + 1) * DH)
        inner = slice(head % width * DH, (head % width + 1) * DH)
        scaled = pages_ref[:, lanes].astype(F32) * factors[:, head : head + 1]
        slab[head // width, :, inner] = scaled.astype(BF16)
    pl.semaphore_wait(barrier, dp + mp - 2)

    my_rows = pl.ds(pl.multiple_of(my_mp * store_rows, store_rows), store_rows)
    for c in range(chunks):
        for k in range(1, mp):
            other = lax.rem(my_mp + k, mp)
            pltpu.make_async_remote_copy(
                src_ref=slab.at[other * chunks + c],
                dst_ref=grouped.at[c, my_rows],
                send_sem=mp_send.at[c],
                recv_sem=mp_recv.at[c],
                device_id={"mp": other},
                device_id_type=MESH,
            ).start()
    for c in range(chunks):
        grouped[c, my_rows] = slab[my_mp * chunks + c]

    iota = functools.partial(lax.broadcasted_iota, jnp.int32)
    ahead = iota((slot, pick.shape[1]), 1) - iota((slot, pick.shape[1]), 0)

    @pl.loop(0, dp, unroll=4 if dp % 4 == 0 else 1)
    def _(r):
        prompt_id = fork_ref[r]
        code = jnp.int32(-(1 << 20))
        for i in range(pages_prompt):
            page = table_ref[i, prompt_id]
            code = jnp.where(
                lax.div(page, group_pages) == my_dp, lax.rem(page, group_pages) * slot, code
            )
        codes[r] = code
        pick[pl.ds(pl.multiple_of(r * slot, slot), slot), :] = ones_where(ahead == code)

    def select(out_ref, matrix, operand):
        def body(start, size):
            rows = pl.ds(start, size)
            out_ref[rows, :] = jnp.dot(
                matrix[rows, :], operand, preferred_element_type=F32
            ).astype(out_ref.dtype)

        over_blocks(out_ref.shape[0], body)

    my_slot = pl.ds(pl.multiple_of(my_dp * slot, slot), slot)

    def exchange(c, source, target, send_sem, recv_sem):
        for k in partner_order(dp):
            other = lax.rem(my_dp + k, dp)
            pltpu.make_async_remote_copy(
                src_ref=source.at[c, pl.ds(pl.multiple_of(other * slot, slot), slot)],
                dst_ref=target.at[c, my_slot],
                send_sem=send_sem.at[c],
                recv_sem=recv_sem.at[c],
                device_id={"dp": other},
                device_id_type=MESH,
            ).start()
        target[c, my_slot] = source[c, my_slot]

    def wait_bytes(view, sem):
        pltpu.make_async_copy(view, view, sem).wait()

    dp_rows = pl.ds(0, (dp - 1) * slot)
    mp_rows = pl.ds(0, (mp - 1) * store_rows)
    for c in range(chunks):
        if mp > 1:
            wait_bytes(grouped.at[c, mp_rows], mp_recv.at[c])
        select(outgoing.at[c], pick, grouped[c])
        exchange(c, outgoing, arrived, dp_send, dp_recv)

    my_prompt = fork_ref[my_dp]
    sources = [
        lax.div(table_ref[i, my_prompt], group_pages) * slot for i in range(pages_prompt)
    ]
    ahead = iota((page_rows, dp * slot), 1) - iota((page_rows, dp * slot), 0)
    for c in range(2):
        for i in range(pages_prompt):
            take[pl.ds(c * prompt_len + i * page_rows, page_rows), :] = ones_where(
                ahead == sources[i] + c * page_rows
            )

    lane = iota((1, DH), 1)

    def transposed(out_ref, block, starts, piece):
        wanted = jnp.zeros((1, DH), jnp.int32)
        for i, start in enumerate(starts):
            wanted = jnp.where(lax.div(lane, piece) == i, start, wanted)
        wanted = wanted + lax.rem(lane, piece)

        def body(start, size):
            down = iota((size, DH), 0) + start
            out_ref[pl.ds(start, size), block * DH : (block + 1) * DH] = ones_where(down == wanted)

        over_blocks(out_ref.shape[0], body)

    per_block = DH // page_rows
    for block in range(2 * prompt_len // DH):
        pieces = [divmod(block * per_block + i, pages_prompt) for i in range(per_block)]
        starts = [sources[i] + c * page_rows for c, i in pieces]
        transposed(take_t, block, starts, page_rows)
    per_block = DH // slot
    for block in range(dp * slot // DH):
        starts = [codes[block * per_block + i] for i in range(per_block)]
        transposed(pick_t, block, starts, slot)
    for load in loads:
        load.wait()

    length = length_ref[0]
    live = lax.broadcasted_iota(jnp.int32, (resp_len, DH), 0) < length
    own_shape = (resp_len, 2 * resp_len)
    causal = lax.broadcasted_iota(jnp.int32, own_shape, 0) <= lax.rem(
        lax.broadcasted_iota(jnp.int32, own_shape, 1), resp_len
    )

    def attend(j, prompt):
        lanes = slice(j * DH, (j + 1) * DH)
        keys = jnp.concatenate([prompt[:prompt_len], rkv_buf[0, 0, :, lanes]], 0)
        values = jnp.concatenate([prompt[prompt_len:], rkv_buf[1, 0, :, lanes]], 0)
        keys_t = keys.astype(F32).T.astype(BF16)
        key_grad = jnp.zeros((total, DH), F32)
        value_grad = jnp.zeros((total, DH), F32)
        for first in range(0, group, 2):
            base = (j * group + first) * DH
            heads = [slice(base, base + DH), slice(base + DH, base + 2 * DH)]
            queries = jnp.concatenate([q_buf[:, h] for h in heads], 0)
            grads = jnp.concatenate(
                [jnp.where(live, g_buf[:, h], jnp.zeros((), BF16)) for h in heads], 0
            )
            scores = lax.dot_general(keys, queries, ACROSS, preferred_element_type=F32)
            scores = jnp.concatenate(
                [scores[:prompt_len], jnp.where(causal, scores[prompt_len:], -1e30)], 0
            )
            top = jnp.max(scores, axis=0, keepdims=True)
            powers = jnp.exp2((scores - top) * to_exp2)
            weights = powers * (1.0 / jnp.sum(powers, axis=0, keepdims=True))
            weights_b = weights.astype(BF16)
            grad_weights = lax.dot_general(values, grads, ACROSS, preferred_element_type=F32)
            delta = jnp.sum(weights_b.astype(F32) * grad_weights, axis=0, keepdims=True)
            grad_scores = (weights * (grad_weights - delta)).astype(BF16)
            query_t = jnp.dot(keys_t, grad_scores, preferred_element_type=F32) * inv_root
            query_grad = query_t.T.astype(BF16)
            for i, h in enumerate(heads):
                dq_buf[:, h] = query_grad[i * resp_len : (i + 1) * resp_len]
            key_grad += jnp.dot(grad_scores, queries, preferred_element_type=F32)
            value_grad += jnp.dot(weights_b, grads, preferred_element_type=F32)
        key_grad = key_grad * inv_root
        dkv_buf[0, 0, :, lanes] = key_grad[prompt_len:].astype(BF16)
        dkv_buf[1, 0, :, lanes] = value_grad[prompt_len:].astype(BF16)
        prompt_grad = jnp.concatenate([key_grad[:prompt_len], value_grad[:prompt_len]], 0)
        return prompt_grad.astype(BF16)

    for c in range(chunks):
        wait_bytes(arrived.at[c, dp_rows], dp_recv.at[c])
        prompt = jnp.dot(take[...], arrived[c], preferred_element_type=F32).astype(BF16)
        parts = [
            attend(c * width + i, prompt[:, i * DH : (i + 1) * DH]) for i in range(width)
        ]
        prompt_grad = jnp.concatenate(parts, 1) if width > 1 else parts[0]
        select(back.at[c], take_t, prompt_grad)
        exchange(c, back, returned, rt_send, rt_recv)

    stores = [
        pltpu.make_async_copy(dq_buf, dq_hbm.at[0], out_sem.at[0]),
        pltpu.make_async_copy(dkv_buf, dkv_hbm, out_sem.at[1]),
    ]
    for store in stores:
        store.start()

    def column(m, c):
        return pl.ds(pl.multiple_of((m * chunks + c) * span, span), span)

    for c in range(chunks):
        wait_bytes(returned.at[c, dp_rows], rt_recv.at[c])
        select(summed, pick_t, returned[c])
        for k in range(1, mp):
            other = lax.rem(my_mp + k, mp)
            rows = pl.ds(pl.multiple_of(other * store_rows, store_rows), store_rows)
            part_out[other * chunks + c] = summed[rows, :].astype(BF16)
            pltpu.make_async_remote_copy(
                src_ref=part_out.at[other * chunks + c],
                dst_ref=part_in.at[c, my_mp],
                send_sem=fm_send.at[c],
                recv_sem=fm_recv.at[c],
                device_id={"mp": other},
                device_id_type=MESH,
            ).start()
        pool_buf[:, column(my_mp, c)] = summed[my_rows, :]
    for c in range(chunks):
        if mp > 1:
            wait_bytes(part_in.at[c, pl.ds(0, mp - 1)], fm_recv.at[c])
        for k in range(1, mp):
            other = lax.rem(my_mp + k, mp)
            pool_buf[:, column(other, c)] = part_in[c, other].astype(F32)
    last = pltpu.make_async_copy(pool_buf, pool_hbm, out_sem.at[2])
    last.start()
    for c in range(chunks):
        if mp > 1:
            wait_bytes(grouped.at[c, mp_rows], mp_send.at[c])
            wait_bytes(part_in.at[c, pl.ds(0, mp - 1)], fm_send.at[c])
        wait_bytes(arrived.at[c, dp_rows], dp_send.at[c])
        wait_bytes(returned.at[c, dp_rows], rt_send.at[c])
    for store in stores:
        store.wait()
    last.wait()


def settle(dq_in, dkv_in, pool_in, dq_out, dkv_out, pool_out, sem):
    copies = []

    def piece(source, target):
        copies.append(pltpu.make_async_copy(source, target, sem.at[len(copies)]))

    rows = dq_in.shape[1] // 4
    for i in range(4):
        piece(dq_in.at[:, pl.ds(i * rows, rows)], dq_out.at[:, pl.ds(i * rows, rows)])
    rows = pool_in.shape[0] // 4
    for i in range(4):
        piece(pool_in.at[pl.ds(i * rows, rows)], pool_out.at[pl.ds(i * rows, rows)])
    piece(dkv_in, dkv_out)
    for copy in copies:
        copy.start()
    for copy in copies:
        copy.wait()


def per_device(resp_q, resp_kv, d_out, lengths, fork, page_table, pool_pages, pool_scales):
    dp = lax.axis_size("dp")
    mp = lax.axis_size("mp")
    pool_dev, _, page_rows, pool_width = pool_pages.shape
    heads_kv = pool_scales.shape[-1]
    kv = heads_kv // mp
    width = WIDTH if kv % WIDTH == 0 else 1
    chunks, span = kv // width, width * DH
    pages_prompt = page_table.shape[1]
    prompt_len = pages_prompt * page_rows
    resp_len = resp_q.shape[1]
    group = resp_q.shape[2] // DH // kv
    slot = 2 * page_rows
    store_rows = pool_dev * slot
    group_rows = mp * store_rows
    slots = dp * slot

    vmem = pl.BlockSpec(memory_space=pltpu.VMEM)
    smem = pl.BlockSpec(memory_space=pltpu.SMEM)
    hbm = pl.BlockSpec(memory_space=pl.ANY)
    dma = pltpu.SemaphoreType.DMA
    total = prompt_len + resp_len
    out_shape = (
        jax.ShapeDtypeStruct(resp_q.shape, BF16),
        jax.ShapeDtypeStruct(resp_kv.shape, BF16),
        jax.ShapeDtypeStruct((store_rows, pool_width), F32),
    )
    buffers = [
        ((store_rows, pool_width), BF16),
        (resp_q.shape[1:], BF16),
        (d_out.shape[1:], BF16),
        (resp_kv.shape, BF16),
        (resp_q.shape[1:], BF16),
        (resp_kv.shape, BF16),
        ((store_rows, pool_width), F32),
        ((slots, group_rows), BF16),
        ((group_rows, slots), BF16),
        ((2 * prompt_len, slots), BF16),
        ((slots, 2 * prompt_len), BF16),
        ((mp * chunks, store_rows, span), BF16),
        ((chunks, group_rows, span), BF16),
        ((chunks, slots, span), BF16),
        ((chunks, slots, span), BF16),
        ((chunks, slots, span), BF16),
        ((chunks, slots, span), BF16),
        ((group_rows, span), F32),
        ((mp * chunks, store_rows, span), BF16),
        ((chunks, mp, store_rows, span), BF16),
    ]
    results = pl.pallas_call(
        functools.partial(kernel, dp, mp, kv, group, width),
        out_shape=out_shape,
        in_specs=[vmem] + [smem] * 3 + [pl.BlockSpec(memory_space=pltpu.HBM)] * 4,
        out_specs=(hbm, hbm, hbm),
        scratch_shapes=[pltpu.VMEM(shape, kind) for shape, kind in buffers]
        + [pltpu.SMEM((dp,), jnp.int32), dma((4,)), dma((3,))]
        + [dma((chunks,))] * 8,
        compiler_params=pltpu.CompilerParams(
            collective_id=0,
            has_side_effects=True,
            vmem_limit_bytes=56 << 20,
        ),
        cost_estimate=pl.CostEstimate(
            flops=10 * group * kv * resp_len * total * DH,
            bytes_accessed=8 * resp_q.shape[1] * resp_q.shape[2],
            transcendentals=group * kv * resp_len * total,
        ),
    )(
        pool_scales,
        fork,
        page_table.T,
        lengths,
        pool_pages.reshape(store_rows, pool_width),
        resp_q,
        d_out,
        resp_kv,
    )
    d_query, d_kv, d_pool = pl.pallas_call(
        settle,
        out_shape=out_shape,
        in_specs=[hbm] * 3,
        out_specs=(hbm, hbm, hbm),
        scratch_shapes=[dma((9,))],
    )(*results)
    return (d_query, d_kv, d_pool.reshape(pool_pages.shape))


def solution(mesh):
    return jax.shard_map(
        per_device,
        mesh=mesh,
        in_specs=(
            P("dp", None, "mp"),
            P(None, "dp", None, "mp"),
            P("dp", None, "mp"),
            P("dp"),
            P(),
            P(),
            P(("dp", "mp"), None, None, None),
            P(("dp", "mp"), None, None),
        ),
        out_specs=(
            P("dp", None, "mp"),
            P(None, "dp", None, "mp"),
            P(("dp", "mp"), None, None, None),
        ),
        check_vma=False,
    )
```

```python
import functools
import math

import jax
import jax.numpy as jnp
from jax import lax
from jax.experimental import pallas as pl
from jax.experimental.pallas import tpu as pltpu
from jax.sharding import PartitionSpec as P

DH = 128
WIDTH = 2
MESH = pl.DeviceIdType.MESH
BF16 = jnp.bfloat16
F32 = jnp.float32
ACROSS = (((1,), (1,)), ((), ()))


def split_rows(rows):
    size = min(rows, 512)
    while rows % size:
        size //= 2
    return size, rows // size


def over_blocks(rows, body):
    size, count = split_rows(rows)
    if count == 1:
        body(0, size)
    else:

        @pl.loop(0, count)
        def _(b):
            body(pl.multiple_of(b * size, size), size)


def partner_order(count):
    half, quarter = count // 2, count // 4
    order = []
    for i in range(quarter):
        order += [half + i, half + quarter + i, quarter + i]
    rest = [k for k in range(1, count) if k not in order]
    return [k for k in order if 0 < k < count] + rest


def ones_where(hit):
    return jnp.where(hit, 1.0, 0.0).astype(BF16)


def kernel(
    dp,
    mp,
    kv,
    group,
    width,
    scales_ref,
    fork_ref,
    table_ref,
    length_ref,
    pages_hbm,
    q_hbm,
    g_hbm,
    rkv_hbm,
    dq_hbm,
    dkv_hbm,
    pool_hbm,
    pages_ref,
    q_buf,
    g_buf,
    rkv_buf,
    dq_buf,
    dkv_buf,
    pool_buf,
    pick,
    pick_t,
    take,
    take_t,
    slab,
    grouped,
    outgoing,
    arrived,
    back,
    returned,
    summed,
    part_out,
    part_in,
    codes,
    in_sem,
    out_sem,
    mp_send,
    mp_recv,
    dp_send,
    dp_recv,
    rt_send,
    rt_recv,
    fm_send,
    fm_recv,
):
    my_dp = lax.axis_index("dp")
    my_mp = lax.axis_index("mp")
    pool_dev = scales_ref.shape[0]
    store_rows = pages_ref.shape[0]
    slot = store_rows // pool_dev
    page_rows = slot // 2
    group_pages = mp * pool_dev
    pages_prompt = table_ref.shape[0]
    resp_len = q_buf.shape[0]
    prompt_len = pages_prompt * page_rows
    total = prompt_len + resp_len
    chunks = kv // width
    span = width * DH
    inv_root = 1.0 / DH**0.5
    to_exp2 = inv_root * math.log2(math.e)

    pages_load = pltpu.make_async_copy(pages_hbm, pages_ref, in_sem.at[3])
    pages_load.start()
    barrier = pltpu.get_barrier_semaphore()

    @pl.loop(1, dp)
    def _(k):
        pl.semaphore_signal(
            barrier, inc=1, device_id={"dp": lax.rem(my_dp + k, dp)}, device_id_type=MESH
        )

    for k in range(1, mp):
        pl.semaphore_signal(
            barrier, inc=1, device_id={"mp": lax.rem(my_mp + k, mp)}, device_id_type=MESH
        )

    loads = [
        pltpu.make_async_copy(rkv_hbm, rkv_buf, in_sem.at[0]),
        pltpu.make_async_copy(q_hbm.at[0], q_buf, in_sem.at[1]),
        pltpu.make_async_copy(g_hbm.at[0], g_buf, in_sem.at[2]),
    ]
    for load in loads:
        load.start()

    factors = []
    for n in range(pool_dev):
        pair = scales_ref[n].astype(F32)
        for c in range(2):
            factors.append(jnp.broadcast_to(pair[c : c + 1, :], (page_rows, mp * kv)))
    factors = jnp.concatenate(factors, 0)
    pages_load.wait()
    for head in range(mp * kv):
        lanes = slice(head * DH, (head + 1) * DH)
        inner = slice(head % width * DH, (head % width + 1) * DH)
        scaled = pages_ref[:, lanes].astype(F32) * factors[:, head : head + 1]
        slab[head // width, :, inner] = scaled.astype(BF16)
    pl.semaphore_wait(barrier, dp + mp - 2)

    my_rows = pl.ds(pl.multiple_of(my_mp * store_rows, store_rows), store_rows)
    for c in range(chunks):
        for k in range(1, mp):
            other = lax.rem(my_mp + k, mp)
            pltpu.make_async_remote_copy(
                src_ref=slab.at[other * chunks + c],
                dst_ref=grouped.at[c, my_rows],
                send_sem=mp_send.at[c],
                recv_sem=mp_recv.at[c],
                device_id={"mp": other},
                device_id_type=MESH,
            ).start()
    for c in range(chunks):
        grouped[c, my_rows] = slab[my_mp * chunks + c]

    iota = functools.partial(lax.broadcasted_iota, jnp.int32)
    ahead = iota((slot, pick.shape[1]), 1) - iota((slot, pick.shape[1]), 0)

    @pl.loop(0, dp, unroll=4 if dp % 4 == 0 else 1)
    def _(r):
        prompt_id = fork_ref[r]
        code = jnp.int32(-(1 << 20))
        for i in range(pages_prompt):
            page = table_ref[i, prompt_id]
            code = jnp.where(
                lax.div(page, group_pages) == my_dp, lax.rem(page, group_pages) * slot, code
            )
        codes[r] = code
        pick[pl.ds(pl.multiple_of(r * slot, slot), slot), :] = ones_where(ahead == code)

    def select(out_ref, matrix, operand):
        def body(start, size):
            rows = pl.ds(start, size)
            out_ref[rows, :] = jnp.dot(
                matrix[rows, :], operand, preferred_element_type=F32
            ).astype(out_ref.dtype)

        over_blocks(out_ref.shape[0], body)

    my_slot = pl.ds(pl.multiple_of(my_dp * slot, slot), slot)

    def exchange(c, source, target, send_sem, recv_sem):
        for k in partner_order(dp):
            other = lax.rem(my_dp + k, dp)
            pltpu.make_async_remote_copy(
                src_ref=source.at[c, pl.ds(pl.multiple_of(other * slot, slot), slot)],
                dst_ref=target.at[c, my_slot],
                send_sem=send_sem.at[c],
                recv_sem=recv_sem.at[c],
                device_id={"dp": other},
                device_id_type=MESH,
            ).start()
        target[c, my_slot] = source[c, my_slot]

    def wait_bytes(view, sem):
        pltpu.make_async_copy(view, view, sem).wait()

    dp_rows = pl.ds(0, (dp - 1) * slot)
    mp_rows = pl.ds(0, (mp - 1) * store_rows)
    for c in range(chunks):
        if mp > 1:
            wait_bytes(grouped.at[c, mp_rows], mp_recv.at[c])
        select(outgoing.at[c], pick, grouped[c])
        exchange(c, outgoing, arrived, dp_send, dp_recv)

    my_prompt = fork_ref[my_dp]
    sources = [
        lax.div(table_ref[i, my_prompt], group_pages) * slot for i in range(pages_prompt)
    ]
    ahead = iota((page_rows, dp * slot), 1) - iota((page_rows, dp * slot), 0)
    for c in range(2):
        for i in range(pages_prompt):
            take[pl.ds(c * prompt_len + i * page_rows, page_rows), :] = ones_where(
                ahead == sources[i] + c * page_rows
            )

    lane = iota((1, DH), 1)

    def transposed(out_ref, block, starts, piece):
        wanted = jnp.zeros((1, DH), jnp.int32)
        for i, start in enumerate(starts):
            wanted = jnp.where(lax.div(lane, piece) == i, start, wanted)
        wanted = wanted + lax.rem(lane, piece)

        def body(start, size):
            down = iota((size, DH), 0) + start
            out_ref[pl.ds(start, size), block * DH : (block + 1) * DH] = ones_where(down == wanted)

        over_blocks(out_ref.shape[0], body)

    per_block = DH // page_rows
    for block in range(2 * prompt_len // DH):
        pieces = [divmod(block * per_block + i, pages_prompt) for i in range(per_block)]
        starts = [sources[i] + c * page_rows for c, i in pieces]
        transposed(take_t, block, starts, page_rows)
    per_block = DH // slot
    for block in range(dp * slot // DH):
        starts = [codes[block * per_block + i] for i in range(per_block)]
        transposed(pick_t, block, starts, slot)
    for load in loads:
        load.wait()

    length = length_ref[0]
    live = lax.broadcasted_iota(jnp.int32, (resp_len, DH), 0) < length
    own_shape = (resp_len, 2 * resp_len)
    causal = lax.broadcasted_iota(jnp.int32, own_shape, 0) <= lax.rem(
        lax.broadcasted_iota(jnp.int32, own_shape, 1), resp_len
    )

    def attend(j, prompt):
        lanes = slice(j * DH, (j + 1) * DH)
        keys = jnp.concatenate([prompt[:prompt_len], rkv_buf[0, 0, :, lanes]], 0)
        values = jnp.concatenate([prompt[prompt_len:], rkv_buf[1, 0, :, lanes]], 0)
        keys_t = keys.astype(F32).T.astype(BF16)
        key_grad = jnp.zeros((total, DH), F32)
        value_grad = jnp.zeros((total, DH), F32)
        for first in range(0, group, 2):
            base = (j * group + first) * DH
            heads = [slice(base, base + DH), slice(base + DH, base + 2 * DH)]
            queries = jnp.concatenate([q_buf[:, h] for h in heads], 0)
            grads = jnp.concatenate(
                [jnp.where(live, g_buf[:, h], jnp.zeros((), BF16)) for h in heads], 0
            )
            scores = lax.dot_general(keys, queries, ACROSS, preferred_element_type=F32)
            scores = jnp.concatenate(
                [scores[:prompt_len], jnp.where(causal, scores[prompt_len:], -1e30)], 0
            )
            top = jnp.max(scores, axis=0, keepdims=True)
            powers = jnp.exp2((scores - top) * to_exp2)
            weights = powers * (1.0 / jnp.sum(powers, axis=0, keepdims=True))
            weights_b = weights.astype(BF16)
            grad_weights = lax.dot_general(values, grads, ACROSS, preferred_element_type=F32)
            delta = jnp.sum(weights_b.astype(F32) * grad_weights, axis=0, keepdims=True)
            grad_scores = (weights * (grad_weights - delta)).astype(BF16)
            query_t = jnp.dot(keys_t, grad_scores, preferred_element_type=F32) * inv_root
            query_grad = query_t.T.astype(BF16)
            for i, h in enumerate(heads):
                dq_buf[:, h] = query_grad[i * resp_len : (i + 1) * resp_len]
            key_grad += jnp.dot(grad_scores, queries, preferred_element_type=F32)
            value_grad += jnp.dot(weights_b, grads, preferred_element_type=F32)
        key_grad = key_grad * inv_root
        dkv_buf[0, 0, :, lanes] = key_grad[prompt_len:].astype(BF16)
        dkv_buf[1, 0, :, lanes] = value_grad[prompt_len:].astype(BF16)
        prompt_grad = jnp.concatenate([key_grad[:prompt_len], value_grad[:prompt_len]], 0)
        return prompt_grad.astype(BF16)

    for c in range(chunks):
        wait_bytes(arrived.at[c, dp_rows], dp_recv.at[c])
        prompt = jnp.dot(take[...], arrived[c], preferred_element_type=F32).astype(BF16)
        parts = [
            attend(c * width + i, prompt[:, i * DH : (i + 1) * DH]) for i in range(width)
        ]
        prompt_grad = jnp.concatenate(parts, 1) if width > 1 else parts[0]
        select(back.at[c], take_t, prompt_grad)
        exchange(c, back, returned, rt_send, rt_recv)

    stores = [
        pltpu.make_async_copy(dq_buf, dq_hbm.at[0], out_sem.at[0]),
        pltpu.make_async_copy(dkv_buf, dkv_hbm, out_sem.at[1]),
    ]
    for store in stores:
        store.start()

    def column(m, c):
        return pl.ds(pl.multiple_of((m * chunks + c) * span, span), span)

    for c in range(chunks):
        wait_bytes(returned.at[c, dp_rows], rt_recv.at[c])
        select(summed, pick_t, returned[c])
        for k in range(1, mp):
            other = lax.rem(my_mp + k, mp)
            rows = pl.ds(pl.multiple_of(other * store_rows, store_rows), store_rows)
            part_out[other * chunks + c] = summed[rows, :].astype(BF16)
            pltpu.make_async_remote_copy(
                src_ref=part_out.at[other * chunks + c],
                dst_ref=part_in.at[c, my_mp],
                send_sem=fm_send.at[c],
                recv_sem=fm_recv.at[c],
                device_id={"mp": other},
                device_id_type=MESH,
            ).start()
        pool_buf[:, column(my_mp, c)] = summed[my_rows, :]
    for c in range(chunks):
        if mp > 1:
            wait_bytes(part_in.at[c, pl.ds(0, mp - 1)], fm_recv.at[c])
        for k in range(1, mp):
            other = lax.rem(my_mp + k, mp)
            pool_buf[:, column(other, c)] = part_in[c, other].astype(F32)
    last = pltpu.make_async_copy(pool_buf, pool_hbm, out_sem.at[2])
    last.start()
    for c in range(chunks):
        if mp > 1:
            wait_bytes(grouped.at[c, mp_rows], mp_send.at[c])
            wait_bytes(part_in.at[c, pl.ds(0, mp - 1)], fm_send.at[c])
        wait_bytes(arrived.at[c, dp_rows], dp_send.at[c])
        wait_bytes(returned.at[c, dp_rows], rt_send.at[c])
    for store in stores:
        store.wait()
    last.wait()


def settle(dq_in, dkv_in, pool_in, dq_out, dkv_out, pool_out, dq_buf, dkv_buf, pool_buf, sem):
    pieces = []
    rows = dq_in.shape[1] // 4
    for i in range(4):
        at = (slice(None), pl.ds(i * rows, rows))
        pieces.append((dq_in.at[at], dq_buf.at[at], dq_out.at[at]))
    rows = pool_in.shape[0] // 4
    for i in range(4):
        at = pl.ds(i * rows, rows)
        pieces.append((pool_in.at[at], pool_buf.at[at], pool_out.at[at]))
    pieces.append((dkv_in, dkv_buf, dkv_out))
    reads, writes = [], []
    for i, (source, middle, target) in enumerate(pieces):
        reads.append(pltpu.make_async_copy(source, middle, sem.at[0, i]))
        writes.append(pltpu.make_async_copy(middle, target, sem.at[1, i]))
    for read in reads:
        read.start()
    for read, write in zip(reads, writes):
        read.wait()
        write.start()
    for write in writes:
        write.wait()


def per_device(resp_q, resp_kv, d_out, lengths, fork, page_table, pool_pages, pool_scales):
    dp = lax.axis_size("dp")
    mp = lax.axis_size("mp")
    pool_dev, _, page_rows, pool_width = pool_pages.shape
    heads_kv = pool_scales.shape[-1]
    kv = heads_kv // mp
    width = WIDTH if kv % WIDTH == 0 else 1
    chunks, span = kv // width, width * DH
    pages_prompt = page_table.shape[1]
    prompt_len = pages_prompt * page_rows
    resp_len = resp_q.shape[1]
    group = resp_q.shape[2] // DH // kv
    slot = 2 * page_rows
    store_rows = pool_dev * slot
    group_rows = mp * store_rows
    slots = dp * slot

    vmem = pl.BlockSpec(memory_space=pltpu.VMEM)
    smem = pl.BlockSpec(memory_space=pltpu.SMEM)
    hbm = pl.BlockSpec(memory_space=pl.ANY)
    dma = pltpu.SemaphoreType.DMA
    total = prompt_len + resp_len
    out_shape = (
        jax.ShapeDtypeStruct(resp_q.shape, BF16),
        jax.ShapeDtypeStruct(resp_kv.shape, BF16),
        jax.ShapeDtypeStruct((store_rows, pool_width), F32),
    )
    buffers = [
        ((store_rows, pool_width), BF16),
        (resp_q.shape[1:], BF16),
        (d_out.shape[1:], BF16),
        (resp_kv.shape, BF16),
        (resp_q.shape[1:], BF16),
        (resp_kv.shape, BF16),
        ((store_rows, pool_width), F32),
        ((slots, group_rows), BF16),
        ((group_rows, slots), BF16),
        ((2 * prompt_len, slots), BF16),
        ((slots, 2 * prompt_len), BF16),
        ((mp * chunks, store_rows, span), BF16),
        ((chunks, group_rows, span), BF16),
        ((chunks, slots, span), BF16),
        ((chunks, slots, span), BF16),
        ((chunks, slots, span), BF16),
        ((chunks, slots, span), BF16),
        ((group_rows, span), F32),
        ((mp * chunks, store_rows, span), BF16),
        ((chunks, mp, store_rows, span), BF16),
    ]
    results = pl.pallas_call(
        functools.partial(kernel, dp, mp, kv, group, width),
        out_shape=out_shape,
        in_specs=[vmem] + [smem] * 3 + [pl.BlockSpec(memory_space=pltpu.HBM)] * 4,
        out_specs=(hbm, hbm, hbm),
        scratch_shapes=[pltpu.VMEM(shape, kind) for shape, kind in buffers]
        + [pltpu.SMEM((dp,), jnp.int32), dma((4,)), dma((3,))]
        + [dma((chunks,))] * 8,
        compiler_params=pltpu.CompilerParams(
            collective_id=0,
            has_side_effects=True,
            vmem_limit_bytes=56 << 20,
        ),
        cost_estimate=pl.CostEstimate(
            flops=10 * group * kv * resp_len * total * DH,
            bytes_accessed=8 * resp_q.shape[1] * resp_q.shape[2],
            transcendentals=group * kv * resp_len * total,
        ),
    )(
        pool_scales,
        fork,
        page_table.T,
        lengths,
        pool_pages.reshape(store_rows, pool_width),
        resp_q,
        d_out,
        resp_kv,
    )
    d_query, d_kv, d_pool = pl.pallas_call(
        settle,
        out_shape=out_shape,
        in_specs=[hbm] * 3,
        out_specs=(hbm, hbm, hbm),
        scratch_shapes=[pltpu.VMEM(o.shape, o.dtype) for o in out_shape] + [dma((2, 9))],
        compiler_params=pltpu.CompilerParams(vmem_limit_bytes=56 << 20),
    )(*results)
    return (d_query, d_kv, d_pool.reshape(pool_pages.shape))


def solution(mesh):
    return jax.shard_map(
        per_device,
        mesh=mesh,
        in_specs=(
            P("dp", None, "mp"),
            P(None, "dp", None, "mp"),
            P("dp", None, "mp"),
            P("dp"),
            P(),
            P(),
            P(("dp", "mp"), None, None, None),
            P(("dp", "mp"), None, None),
        ),
        out_specs=(
            P("dp", None, "mp"),
            P(None, "dp", None, "mp"),
            P(("dp", "mp"), None, None, None),
        ),
        check_vma=False,
    )
```

```python
import functools
import math

import jax
import jax.numpy as jnp
from jax import lax
from jax.experimental import pallas as pl
from jax.experimental.pallas import tpu as pltpu
from jax.sharding import PartitionSpec as P

DH = 128
WIDTH = 1
MESH = pl.DeviceIdType.MESH
BF16 = jnp.bfloat16
F32 = jnp.float32
ACROSS = (((1,), (1,)), ((), ()))


def split_rows(rows):
    size = min(rows, 512)
    while rows % size:
        size //= 2
    return size, rows // size


def over_blocks(rows, body):
    size, count = split_rows(rows)
    if count == 1:
        body(0, size)
    else:

        @pl.loop(0, count)
        def _(b):
            body(pl.multiple_of(b * size, size), size)


def partner_order(count):
    half, quarter = count // 2, count // 4
    order = []
    for i in range(quarter):
        order += [half + i, half + quarter + i, quarter + i]
    rest = [k for k in range(1, count) if k not in order]
    return [k for k in order if 0 < k < count] + rest


def ones_where(hit):
    return jnp.where(hit, 1.0, 0.0).astype(BF16)


def kernel(
    dp,
    mp,
    kv,
    group,
    width,
    scales_ref,
    fork_ref,
    table_ref,
    length_ref,
    pages_hbm,
    q_hbm,
    g_hbm,
    rkv_hbm,
    dq_hbm,
    dkv_hbm,
    pool_hbm,
    pages_ref,
    q_buf,
    g_buf,
    rkv_buf,
    dq_buf,
    dkv_buf,
    pool_buf,
    pick,
    pick_t,
    take,
    take_t,
    slab,
    grouped,
    outgoing,
    arrived,
    back,
    returned,
    summed,
    part_out,
    part_in,
    queries,
    grads,
    scores,
    grad_weights,
    weights_b,
    grad_scores,
    codes,
    in_sem,
    out_sem,
    mp_send,
    mp_recv,
    dp_send,
    dp_recv,
    rt_send,
    rt_recv,
    fm_send,
    fm_recv,
):
    my_dp = lax.axis_index("dp")
    my_mp = lax.axis_index("mp")
    pool_dev = scales_ref.shape[0]
    store_rows = pages_ref.shape[0]
    slot = store_rows // pool_dev
    page_rows = slot // 2
    group_pages = mp * pool_dev
    pages_prompt = table_ref.shape[0]
    resp_len = q_buf.shape[0]
    prompt_len = pages_prompt * page_rows
    total = prompt_len + resp_len
    chunks = kv // width
    span = width * DH
    inv_root = 1.0 / DH**0.5
    to_exp2 = inv_root * math.log2(math.e)

    pages_load = pltpu.make_async_copy(pages_hbm, pages_ref, in_sem.at[3])
    pages_load.start()
    barrier = pltpu.get_barrier_semaphore()

    @pl.loop(1, dp)
    def _(k):
        pl.semaphore_signal(
            barrier, inc=1, device_id={"dp": lax.rem(my_dp + k, dp)}, device_id_type=MESH
        )

    for k in range(1, mp):
        pl.semaphore_signal(
            barrier, inc=1, device_id={"mp": lax.rem(my_mp + k, mp)}, device_id_type=MESH
        )

    loads = [
        pltpu.make_async_copy(rkv_hbm, rkv_buf, in_sem.at[0]),
        pltpu.make_async_copy(q_hbm.at[0], q_buf, in_sem.at[1]),
        pltpu.make_async_copy(g_hbm.at[0], g_buf, in_sem.at[2]),
    ]
    for load in loads:
        load.start()

    factors = []
    for n in range(pool_dev):
        pair = scales_ref[n].astype(F32)
        for c in range(2):
            factors.append(jnp.broadcast_to(pair[c : c + 1, :], (page_rows, mp * kv)))
    factors = jnp.concatenate(factors, 0)
    pages_load.wait()
    for head in range(mp * kv):
        lanes = slice(head * DH, (head + 1) * DH)
        inner = slice(head % width * DH, (head % width + 1) * DH)
        scaled = pages_ref[:, lanes].astype(F32) * factors[:, head : head + 1]
        slab[head // width, :, inner] = scaled.astype(BF16)
    pl.semaphore_wait(barrier, dp + mp - 2)

    my_rows = pl.ds(pl.multiple_of(my_mp * store_rows, store_rows), store_rows)
    for c in range(chunks):
        for k in range(1, mp):
            other = lax.rem(my_mp + k, mp)
            pltpu.make_async_remote_copy(
                src_ref=slab.at[other * chunks + c],
                dst_ref=grouped.at[c, my_rows],
                send_sem=mp_send.at[c],
                recv_sem=mp_recv.at[c],
                device_id={"mp": other},
                device_id_type=MESH,
            ).start()
    for c in range(chunks):
        grouped[c, my_rows] = slab[my_mp * chunks + c]

    iota = functools.partial(lax.broadcasted_iota, jnp.int32)
    ahead = iota((slot, pick.shape[1]), 1) - iota((slot, pick.shape[1]), 0)

    @pl.loop(0, dp, unroll=4 if dp % 4 == 0 else 1)
    def _(r):
        prompt_id = fork_ref[r]
        code = jnp.int32(-(1 << 20))
        for i in range(pages_prompt):
            page = table_ref[i, prompt_id]
            code = jnp.where(
                lax.div(page, group_pages) == my_dp, lax.rem(page, group_pages) * slot, code
            )
        codes[r] = code
        pick[pl.ds(pl.multiple_of(r * slot, slot), slot), :] = ones_where(ahead == code)

    def select(out_ref, matrix, operand):
        def body(start, size):
            rows = pl.ds(start, size)
            out_ref[rows, :] = jnp.dot(
                matrix[rows, :], operand, preferred_element_type=F32
            ).astype(out_ref.dtype)

        over_blocks(out_ref.shape[0], body)

    my_slot = pl.ds(pl.multiple_of(my_dp * slot, slot), slot)

    def exchange(c, source, target, send_sem, recv_sem):
        for k in partner_order(dp):
            other = lax.rem(my_dp + k, dp)
            pltpu.make_async_remote_copy(
                src_ref=source.at[c, pl.ds(pl.multiple_of(other * slot, slot), slot)],
                dst_ref=target.at[c, my_slot],
                send_sem=send_sem.at[c],
                recv_sem=recv_sem.at[c],
                device_id={"dp": other},
                device_id_type=MESH,
            ).start()
        target[c, my_slot] = source[c, my_slot]

    def wait_bytes(view, sem):
        pltpu.make_async_copy(view, view, sem).wait()

    dp_rows = pl.ds(0, (dp - 1) * slot)
    mp_rows = pl.ds(0, (mp - 1) * store_rows)
    for c in range(chunks):
        if mp > 1:
            wait_bytes(grouped.at[c, mp_rows], mp_recv.at[c])
        select(outgoing.at[c], pick, grouped[c])
        exchange(c, outgoing, arrived, dp_send, dp_recv)

    my_prompt = fork_ref[my_dp]
    sources = [
        lax.div(table_ref[i, my_prompt], group_pages) * slot for i in range(pages_prompt)
    ]
    ahead = iota((page_rows, dp * slot), 1) - iota((page_rows, dp * slot), 0)
    for c in range(2):
        for i in range(pages_prompt):
            take[pl.ds(c * prompt_len + i * page_rows, page_rows), :] = ones_where(
                ahead == sources[i] + c * page_rows
            )

    lane = iota((1, DH), 1)

    def transposed(out_ref, block, starts, piece):
        wanted = jnp.zeros((1, DH), jnp.int32)
        for i, start in enumerate(starts):
            wanted = jnp.where(lax.div(lane, piece) == i, start, wanted)
        wanted = wanted + lax.rem(lane, piece)

        def body(start, size):
            down = iota((size, DH), 0) + start
            out_ref[pl.ds(start, size), block * DH : (block + 1) * DH] = ones_where(down == wanted)

        over_blocks(out_ref.shape[0], body)

    per_block = DH // page_rows
    for block in range(2 * prompt_len // DH):
        pieces = [divmod(block * per_block + i, pages_prompt) for i in range(per_block)]
        starts = [sources[i] + c * page_rows for c, i in pieces]
        transposed(take_t, block, starts, page_rows)
    per_block = DH // slot
    for block in range(dp * slot // DH):
        starts = [codes[block * per_block + i] for i in range(per_block)]
        transposed(pick_t, block, starts, slot)
    for load in loads:
        load.wait()

    live = iota((resp_len, DH), 0) < length_ref[0]
    for h in range(kv * group):
        lanes = slice(h * DH, (h + 1) * DH)
        rows = pl.ds(h % group * resp_len, resp_len)
        queries[h // group, rows, :] = q_buf[:, lanes]
        grads[h // group, rows, :] = jnp.where(live, g_buf[:, lanes], jnp.zeros((), BF16))
    causal = iota((resp_len, resp_len), 0) <= iota((resp_len, resp_len), 1)

    def attend(j, prompt):
        lanes = slice(j * DH, (j + 1) * DH)
        keys = jnp.concatenate([prompt[:prompt_len], rkv_buf[0, 0, :, lanes]], 0)
        values = jnp.concatenate([prompt[prompt_len:], rkv_buf[1, 0, :, lanes]], 0)
        keys_t = keys.astype(F32).T.astype(BF16)
        scores[...] = lax.dot_general(keys, queries[j], ACROSS, preferred_element_type=F32)
        grad_weights[...] = lax.dot_general(
            values, grads[j], ACROSS, preferred_element_type=F32
        )
        for i in range(group):
            across = slice(i * resp_len, (i + 1) * resp_len)
            block = jnp.concatenate(
                [
                    scores[:prompt_len, across],
                    jnp.where(causal, scores[prompt_len:, across], -1e30),
                ],
                0,
            )
            top = jnp.max(block, axis=0, keepdims=True)
            powers = jnp.exp2((block - top) * to_exp2)
            weights = powers * (1.0 / jnp.sum(powers, axis=0, keepdims=True))
            rounded = weights.astype(BF16)
            change = grad_weights[:, across]
            delta = jnp.sum(rounded.astype(F32) * change, axis=0, keepdims=True)
            weights_b[:, across] = rounded
            grad_scores[:, across] = (weights * (change - delta)).astype(BF16)
        query_t = jnp.dot(keys_t, grad_scores[...], preferred_element_type=F32) * inv_root
        for i in range(group):
            h = j * group + i
            dq_buf[:, h * DH : (h + 1) * DH] = query_t[
                :, i * resp_len : (i + 1) * resp_len
            ].T.astype(BF16)
        key_grad = (
            jnp.dot(grad_scores[...], queries[j], preferred_element_type=F32) * inv_root
        )
        value_grad = jnp.dot(weights_b[...], grads[j], preferred_element_type=F32)
        dkv_buf[0, 0, :, lanes] = key_grad[prompt_len:].astype(BF16)
        dkv_buf[1, 0, :, lanes] = value_grad[prompt_len:].astype(BF16)
        prompt_grad = jnp.concatenate([key_grad[:prompt_len], value_grad[:prompt_len]], 0)
        return prompt_grad.astype(BF16)

    for c in range(chunks):
        wait_bytes(arrived.at[c, dp_rows], dp_recv.at[c])
        prompt = jnp.dot(take[...], arrived[c], preferred_element_type=F32).astype(BF16)
        parts = [
            attend(c * width + i, prompt[:, i * DH : (i + 1) * DH]) for i in range(width)
        ]
        prompt_grad = jnp.concatenate(parts, 1) if width > 1 else parts[0]
        select(back.at[c], take_t, prompt_grad)
        exchange(c, back, returned, rt_send, rt_recv)

    stores = [
        pltpu.make_async_copy(dq_buf, dq_hbm.at[0], out_sem.at[0]),
        pltpu.make_async_copy(dkv_buf, dkv_hbm, out_sem.at[1]),
    ]
    for store in stores:
        store.start()

    def column(m, c):
        return pl.ds(pl.multiple_of((m * chunks + c) * span, span), span)

    for c in range(chunks):
        wait_bytes(returned.at[c, dp_rows], rt_recv.at[c])
        select(summed, pick_t, returned[c])
        for k in range(1, mp):
            other = lax.rem(my_mp + k, mp)
            rows = pl.ds(pl.multiple_of(other * store_rows, store_rows), store_rows)
            part_out[other * chunks + c] = summed[rows, :].astype(BF16)
            pltpu.make_async_remote_copy(
                src_ref=part_out.at[other * chunks + c],
                dst_ref=part_in.at[c, my_mp],
                send_sem=fm_send.at[c],
                recv_sem=fm_recv.at[c],
                device_id={"mp": other},
                device_id_type=MESH,
            ).start()
        pool_buf[:, column(my_mp, c)] = summed[my_rows, :]
    for c in range(chunks):
        if mp > 1:
            wait_bytes(part_in.at[c, pl.ds(0, mp - 1)], fm_recv.at[c])
        for k in range(1, mp):
            other = lax.rem(my_mp + k, mp)
            pool_buf[:, column(other, c)] = part_in[c, other].astype(F32)
    last = pltpu.make_async_copy(pool_buf, pool_hbm, out_sem.at[2])
    last.start()
    for c in range(chunks):
        if mp > 1:
            wait_bytes(grouped.at[c, mp_rows], mp_send.at[c])
            wait_bytes(part_in.at[c, pl.ds(0, mp - 1)], fm_send.at[c])
        wait_bytes(arrived.at[c, dp_rows], dp_send.at[c])
        wait_bytes(returned.at[c, dp_rows], rt_send.at[c])
    for store in stores:
        store.wait()
    last.wait()


def settle(dq_in, dkv_in, pool_in, dq_out, dkv_out, pool_out, dq_buf, dkv_buf, pool_buf, sem):
    pieces = []
    rows = dq_in.shape[1] // 4
    for i in range(4):
        at = (slice(None), pl.ds(i * rows, rows))
        pieces.append((dq_in.at[at], dq_buf.at[at], dq_out.at[at]))
    rows = pool_in.shape[0] // 4
    for i in range(4):
        at = pl.ds(i * rows, rows)
        pieces.append((pool_in.at[at], pool_buf.at[at], pool_out.at[at]))
    pieces.append((dkv_in, dkv_buf, dkv_out))
    reads, writes = [], []
    for i, (source, middle, target) in enumerate(pieces):
        reads.append(pltpu.make_async_copy(source, middle, sem.at[0, i]))
        writes.append(pltpu.make_async_copy(middle, target, sem.at[1, i]))
    for read in reads:
        read.start()
    for read, write in zip(reads, writes):
        read.wait()
        write.start()
    for write in writes:
        write.wait()


def per_device(resp_q, resp_kv, d_out, lengths, fork, page_table, pool_pages, pool_scales):
    dp = lax.axis_size("dp")
    mp = lax.axis_size("mp")
    pool_dev, _, page_rows, pool_width = pool_pages.shape
    heads_kv = pool_scales.shape[-1]
    kv = heads_kv // mp
    width = WIDTH if kv % WIDTH == 0 else 1
    chunks, span = kv // width, width * DH
    pages_prompt = page_table.shape[1]
    prompt_len = pages_prompt * page_rows
    resp_len = resp_q.shape[1]
    group = resp_q.shape[2] // DH // kv
    slot = 2 * page_rows
    store_rows = pool_dev * slot
    group_rows = mp * store_rows
    slots = dp * slot

    vmem = pl.BlockSpec(memory_space=pltpu.VMEM)
    smem = pl.BlockSpec(memory_space=pltpu.SMEM)
    hbm = pl.BlockSpec(memory_space=pl.ANY)
    dma = pltpu.SemaphoreType.DMA
    total = prompt_len + resp_len
    out_shape = (
        jax.ShapeDtypeStruct(resp_q.shape, BF16),
        jax.ShapeDtypeStruct(resp_kv.shape, BF16),
        jax.ShapeDtypeStruct((store_rows, pool_width), F32),
    )
    buffers = [
        ((store_rows, pool_width), BF16),
        (resp_q.shape[1:], BF16),
        (d_out.shape[1:], BF16),
        (resp_kv.shape, BF16),
        (resp_q.shape[1:], BF16),
        (resp_kv.shape, BF16),
        ((store_rows, pool_width), F32),
        ((slots, group_rows), BF16),
        ((group_rows, slots), BF16),
        ((2 * prompt_len, slots), BF16),
        ((slots, 2 * prompt_len), BF16),
        ((mp * chunks, store_rows, span), BF16),
        ((chunks, group_rows, span), BF16),
        ((chunks, slots, span), BF16),
        ((chunks, slots, span), BF16),
        ((chunks, slots, span), BF16),
        ((chunks, slots, span), BF16),
        ((group_rows, span), F32),
        ((mp * chunks, store_rows, span), BF16),
        ((chunks, mp, store_rows, span), BF16),
        ((kv, group * resp_len, DH), BF16),
        ((kv, group * resp_len, DH), BF16),
        ((total, group * resp_len), F32),
        ((total, group * resp_len), F32),
        ((total, group * resp_len), BF16),
        ((total, group * resp_len), BF16),
    ]
    results = pl.pallas_call(
        functools.partial(kernel, dp, mp, kv, group, width),
        out_shape=out_shape,
        in_specs=[vmem] + [smem] * 3 + [pl.BlockSpec(memory_space=pltpu.HBM)] * 4,
        out_specs=(hbm, hbm, hbm),
        scratch_shapes=[pltpu.VMEM(shape, kind) for shape, kind in buffers]
        + [pltpu.SMEM((dp,), jnp.int32), dma((4,)), dma((3,))]
        + [dma((chunks,))] * 8,
        compiler_params=pltpu.CompilerParams(
            collective_id=0,
            has_side_effects=True,
            vmem_limit_bytes=56 << 20,
        ),
        cost_estimate=pl.CostEstimate(
            flops=10 * group * kv * resp_len * total * DH,
            bytes_accessed=8 * resp_q.shape[1] * resp_q.shape[2],
            transcendentals=group * kv * resp_len * total,
        ),
    )(
        pool_scales,
        fork,
        page_table.T,
        lengths,
        pool_pages.reshape(store_rows, pool_width),
        resp_q,
        d_out,
        resp_kv,
    )
    d_query, d_kv, d_pool = pl.pallas_call(
        settle,
        out_shape=out_shape,
        in_specs=[hbm] * 3,
        out_specs=(hbm, hbm, hbm),
        scratch_shapes=[pltpu.VMEM(o.shape, o.dtype) for o in out_shape] + [dma((2, 9))],
        compiler_params=pltpu.CompilerParams(vmem_limit_bytes=56 << 20),
    )(*results)
    return (d_query, d_kv, d_pool.reshape(pool_pages.shape))


def solution(mesh):
    return jax.shard_map(
        per_device,
        mesh=mesh,
        in_specs=(
            P("dp", None, "mp"),
            P(None, "dp", None, "mp"),
            P("dp", None, "mp"),
            P("dp"),
            P(),
            P(),
            P(("dp", "mp"), None, None, None),
            P(("dp", "mp"), None, None),
        ),
        out_specs=(
            P("dp", None, "mp"),
            P(None, "dp", None, "mp"),
            P(("dp", "mp"), None, None, None),
        ),
        check_vma=False,
    )
```

```python
import functools
import math

import jax
import jax.numpy as jnp
from jax import lax
from jax.experimental import pallas as pl
from jax.experimental.pallas import tpu as pltpu
from jax.sharding import PartitionSpec as P

DH = 128
MESH = pl.DeviceIdType.MESH
BF16 = jnp.bfloat16
F32 = jnp.float32
ACROSS = (((1,), (1,)), ((), ()))


def split_rows(rows):
    size = min(rows, 512)
    while rows % size:
        size //= 2
    return size, rows // size


def over_blocks(rows, body):
    size, count = split_rows(rows)
    if count == 1:
        body(0, size)
    else:

        @pl.loop(0, count)
        def _(b):
            body(pl.multiple_of(b * size, size), size)


def partner_order(count):
    half, quarter = count // 2, count // 4
    order = []
    for i in range(quarter):
        order += [half + i, half + quarter + i, quarter + i]
    rest = [k for k in range(1, count) if k not in order]
    return [k for k in order if 0 < k < count] + rest


def ones_where(hit):
    return jnp.where(hit, 1.0, 0.0).astype(BF16)


def kernel(
    dp,
    mp,
    kv,
    group,
    scales_ref,
    fork_ref,
    table_ref,
    length_ref,
    pages_hbm,
    q_hbm,
    g_hbm,
    rkv_hbm,
    dq_hbm,
    dkv_hbm,
    pool_hbm,
    pages_ref,
    q_buf,
    g_buf,
    rkv_buf,
    dq_buf,
    dkv_buf,
    pool_buf,
    pick,
    pick_t,
    take,
    take_t,
    slab,
    grouped,
    outgoing,
    arrived,
    back,
    returned,
    summed,
    part_out,
    part_in,
    queries,
    grads,
    scores,
    grad_weights,
    weights_b,
    grad_scores,
    codes,
    in_sem,
    out_sem,
    mp_send,
    mp_recv,
    dp_send,
    dp_recv,
    rt_send,
    rt_recv,
    fm_send,
    fm_recv,
):
    my_dp = lax.axis_index("dp")
    my_mp = lax.axis_index("mp")
    pool_dev = scales_ref.shape[0]
    page_rows = pages_ref.shape[2]
    store_rows = pool_dev * page_rows
    group_pages = mp * pool_dev
    pages_prompt = table_ref.shape[0]
    resp_len = q_buf.shape[0]
    prompt_len = pages_prompt * page_rows
    total = prompt_len + resp_len
    chunks = 2 * kv
    inv_root = 1.0 / DH**0.5
    to_exp2 = inv_root * math.log2(math.e)

    pages_load = pltpu.make_async_copy(pages_hbm, pages_ref, in_sem.at[3])
    pages_load.start()
    barrier = pltpu.get_barrier_semaphore()

    @pl.loop(1, dp)
    def _(k):
        pl.semaphore_signal(
            barrier, inc=1, device_id={"dp": lax.rem(my_dp + k, dp)}, device_id_type=MESH
        )

    for k in range(1, mp):
        pl.semaphore_signal(
            barrier, inc=1, device_id={"mp": lax.rem(my_mp + k, mp)}, device_id_type=MESH
        )

    loads = [
        pltpu.make_async_copy(rkv_hbm, rkv_buf, in_sem.at[0]),
        pltpu.make_async_copy(q_hbm.at[0], q_buf, in_sem.at[1]),
        pltpu.make_async_copy(g_hbm.at[0], g_buf, in_sem.at[2]),
    ]
    for load in loads:
        load.start()

    factors = []
    for n in range(pool_dev):
        pair = scales_ref[n].astype(F32)
        for c in range(2):
            factors.append(jnp.broadcast_to(pair[c : c + 1, :], (page_rows, mp * kv)))
    pages_load.wait()
    for c in range(2):
        column = jnp.concatenate(factors[c::2], 0)
        for head in range(mp * kv):
            stored = pages_ref[:, c, :, head * DH : (head + 1) * DH].reshape(store_rows, DH)
            scaled = stored.astype(F32) * column[:, head : head + 1]
            slab[head * 2 + c] = scaled.astype(BF16)
    pl.semaphore_wait(barrier, dp + mp - 2)

    my_rows = pl.ds(pl.multiple_of(my_mp * store_rows, store_rows), store_rows)
    for c in range(chunks):
        for k in range(1, mp):
            other = lax.rem(my_mp + k, mp)
            pltpu.make_async_remote_copy(
                src_ref=slab.at[other * chunks + c],
                dst_ref=grouped.at[c, my_rows],
                send_sem=mp_send.at[c],
                recv_sem=mp_recv.at[c],
                device_id={"mp": other},
                device_id_type=MESH,
            ).start()
    for c in range(chunks):
        grouped[c, my_rows] = slab[my_mp * chunks + c]

    iota = functools.partial(lax.broadcasted_iota, jnp.int32)
    ahead = iota((page_rows, pick.shape[1]), 1) - iota((page_rows, pick.shape[1]), 0)

    @pl.loop(0, dp, unroll=4 if dp % 4 == 0 else 1)
    def _(r):
        prompt_id = fork_ref[r]
        code = jnp.int32(-(1 << 20))
        for i in range(pages_prompt):
            page = table_ref[i, prompt_id]
            code = jnp.where(
                lax.div(page, group_pages) == my_dp, lax.rem(page, group_pages) * page_rows, code
            )
        codes[r] = code
        pick[pl.ds(pl.multiple_of(r * page_rows, page_rows), page_rows), :] = ones_where(ahead == code)

    def select(out_ref, matrix, operand):
        def body(start, size):
            rows = pl.ds(start, size)
            out_ref[rows, :] = jnp.dot(
                matrix[rows, :], operand, preferred_element_type=F32
            ).astype(out_ref.dtype)

        over_blocks(out_ref.shape[0], body)

    my_slot = pl.ds(pl.multiple_of(my_dp * page_rows, page_rows), page_rows)

    def exchange(c, source, target, send_sem, recv_sem):
        for k in partner_order(dp):
            other = lax.rem(my_dp + k, dp)
            pltpu.make_async_remote_copy(
                src_ref=source.at[c, pl.ds(pl.multiple_of(other * page_rows, page_rows), page_rows)],
                dst_ref=target.at[c, my_slot],
                send_sem=send_sem.at[c],
                recv_sem=recv_sem.at[c],
                device_id={"dp": other},
                device_id_type=MESH,
            ).start()
        target[c, my_slot] = source[c, my_slot]

    def wait_bytes(view, sem):
        pltpu.make_async_copy(view, view, sem).wait()

    dp_rows = pl.ds(0, (dp - 1) * page_rows)
    mp_rows = pl.ds(0, (mp - 1) * store_rows)
    for c in range(chunks):
        if mp > 1:
            wait_bytes(grouped.at[c, mp_rows], mp_recv.at[c])
        select(outgoing.at[c], pick, grouped[c])
        exchange(c, outgoing, arrived, dp_send, dp_recv)

    my_prompt = fork_ref[my_dp]
    sources = [
        lax.div(table_ref[i, my_prompt], group_pages) * page_rows for i in range(pages_prompt)
    ]
    ahead = iota((page_rows, dp * page_rows), 1) - iota((page_rows, dp * page_rows), 0)
    for i in range(pages_prompt):
        take[pl.ds(i * page_rows, page_rows), :] = ones_where(ahead == sources[i])

    lane = iota((1, DH), 1)

    def transposed(out_ref, starts):
        per_block = DH // page_rows
        for block in range(-(-len(starts) // per_block)):
            wanted = jnp.zeros((1, DH), jnp.int32)
            for i, start in enumerate(starts[block * per_block : (block + 1) * per_block]):
                wanted = jnp.where(lax.div(lane, page_rows) == i, start, wanted)
            wanted = wanted + lax.rem(lane, page_rows)
            columns = min(DH, len(starts) * page_rows - block * DH)

            def body(first, size):
                down = iota((size, DH), 0) + first
                out_ref[pl.ds(first, size), block * DH : block * DH + columns] = ones_where(
                    down == wanted
                )[:, :columns]

            over_blocks(out_ref.shape[0], body)

    transposed(take_t, sources)
    transposed(pick_t, [codes[r] for r in range(dp)])
    for load in loads:
        load.wait()

    live = iota((resp_len, DH), 0) < length_ref[0]
    for h in range(kv * group):
        lanes = slice(h * DH, (h + 1) * DH)
        rows = pl.ds(h % group * resp_len, resp_len)
        queries[h // group, rows, :] = q_buf[:, lanes]
        grads[h // group, rows, :] = jnp.where(live, g_buf[:, lanes], jnp.zeros((), BF16))
    causal = iota((resp_len, resp_len), 0) <= iota((resp_len, resp_len), 1)

    def attend(j, prompt_keys, prompt_values):
        lanes = slice(j * DH, (j + 1) * DH)
        keys = jnp.concatenate([prompt_keys, rkv_buf[0, 0, :, lanes]], 0)
        values = jnp.concatenate([prompt_values, rkv_buf[1, 0, :, lanes]], 0)
        keys_t = keys.astype(F32).T.astype(BF16)
        scores[...] = lax.dot_general(keys, queries[j], ACROSS, preferred_element_type=F32)
        grad_weights[...] = lax.dot_general(
            values, grads[j], ACROSS, preferred_element_type=F32
        )
        for i in range(group):
            across = slice(i * resp_len, (i + 1) * resp_len)
            block = jnp.concatenate(
                [
                    scores[:prompt_len, across],
                    jnp.where(causal, scores[prompt_len:, across], -1e30),
                ],
                0,
            )
            top = jnp.max(block, axis=0, keepdims=True)
            powers = jnp.exp2((block - top) * to_exp2)
            weights = powers * (1.0 / jnp.sum(powers, axis=0, keepdims=True))
            rounded = weights.astype(BF16)
            change = grad_weights[:, across]
            delta = jnp.sum(rounded.astype(F32) * change, axis=0, keepdims=True)
            weights_b[:, across] = rounded
            grad_scores[:, across] = (weights * (change - delta)).astype(BF16)
        query_t = jnp.dot(keys_t, grad_scores[...], preferred_element_type=F32) * inv_root
        for i in range(group):
            h = j * group + i
            dq_buf[:, h * DH : (h + 1) * DH] = query_t[
                :, i * resp_len : (i + 1) * resp_len
            ].T.astype(BF16)
        value_grad = jnp.dot(weights_b[...], grads[j], preferred_element_type=F32)
        give_back(2 * j + 1, value_grad)
        key_grad = (
            jnp.dot(grad_scores[...], queries[j], preferred_element_type=F32) * inv_root
        )
        give_back(2 * j, key_grad)
        dkv_buf[0, 0, :, lanes] = key_grad[prompt_len:].astype(BF16)
        dkv_buf[1, 0, :, lanes] = value_grad[prompt_len:].astype(BF16)

    def give_back(q, grad):
        select(back.at[q], take_t, grad[:prompt_len].astype(BF16))
        exchange(q, back, returned, rt_send, rt_recv)

    def prompt_part(q):
        wait_bytes(arrived.at[q, dp_rows], dp_recv.at[q])
        return jnp.dot(take[...], arrived[q], preferred_element_type=F32).astype(BF16)

    for j in range(kv):
        attend(j, prompt_part(2 * j), prompt_part(2 * j + 1))

    stores = [
        pltpu.make_async_copy(dq_buf, dq_hbm.at[0], out_sem.at[0]),
        pltpu.make_async_copy(dkv_buf, dkv_hbm, out_sem.at[1]),
    ]
    for store in stores:
        store.start()

    def settled(m, q, block):
        head = m * kv + q // 2
        at = (slice(None), q % 2, slice(None), pl.ds(pl.multiple_of(head * DH, DH), DH))
        pool_buf[at] = block.reshape(pool_dev, page_rows, DH)
        pltpu.make_async_copy(pool_buf.at[at], pool_hbm.at[at], out_sem.at[2]).start()

    def finish(q):
        if mp > 1:
            wait_bytes(part_in.at[q, pl.ds(0, mp - 1)], fm_recv.at[q])
        for k in range(1, mp):
            other = lax.rem(my_mp + k, mp)
            settled(other, q, part_in[q, other].astype(F32))

    order = [2 * j + c for j in range(kv) for c in (1, 0)]
    for i, q in enumerate(order):
        wait_bytes(returned.at[q, dp_rows], rt_recv.at[q])
        select(summed, pick_t, returned[q])
        for k in range(1, mp):
            other = lax.rem(my_mp + k, mp)
            rows = pl.ds(pl.multiple_of(other * store_rows, store_rows), store_rows)
            part_out[other * chunks + q] = summed[rows, :].astype(BF16)
            pltpu.make_async_remote_copy(
                src_ref=part_out.at[other * chunks + q],
                dst_ref=part_in.at[q, my_mp],
                send_sem=fm_send.at[q],
                recv_sem=fm_recv.at[q],
                device_id={"mp": other},
                device_id_type=MESH,
            ).start()
        settled(my_mp, q, summed[my_rows, :])
        if i > 0:
            finish(order[i - 1])
    finish(order[-1])
    for q in range(chunks):
        if mp > 1:
            wait_bytes(grouped.at[q, mp_rows], mp_send.at[q])
            wait_bytes(part_in.at[q, pl.ds(0, mp - 1)], fm_send.at[q])
        wait_bytes(arrived.at[q, dp_rows], dp_send.at[q])
        wait_bytes(returned.at[q, dp_rows], rt_send.at[q])
    last = pltpu.make_async_copy(pool_buf, pool_hbm, out_sem.at[2])
    for store in stores:
        store.wait()
    last.wait()


def settle(dq_in, dkv_in, pool_in, dq_out, dkv_out, pool_out, dq_buf, dkv_buf, pool_buf, sem):
    pieces = []
    rows = dq_in.shape[1] // 4
    for i in range(4):
        at = (slice(None), pl.ds(i * rows, rows))
        pieces.append((dq_in.at[at], dq_buf.at[at], dq_out.at[at]))
    rows = pool_in.shape[0] // 4
    for i in range(4):
        at = pl.ds(i * rows, rows)
        pieces.append((pool_in.at[at], pool_buf.at[at], pool_out.at[at]))
    pieces.append((dkv_in, dkv_buf, dkv_out))
    reads, writes = [], []
    for i, (source, middle, target) in enumerate(pieces):
        reads.append(pltpu.make_async_copy(source, middle, sem.at[0, i]))
        writes.append(pltpu.make_async_copy(middle, target, sem.at[1, i]))
    for read in reads:
        read.start()
    for read, write in zip(reads, writes):
        read.wait()
        write.start()
    for write in writes:
        write.wait()


def per_device(resp_q, resp_kv, d_out, lengths, fork, page_table, pool_pages, pool_scales):
    dp = lax.axis_size("dp")
    mp = lax.axis_size("mp")
    pool_dev, _, page_rows, _ = pool_pages.shape
    heads_kv = pool_scales.shape[-1]
    kv = heads_kv // mp
    chunks = 2 * kv
    pages_prompt = page_table.shape[1]
    prompt_len = pages_prompt * page_rows
    resp_len = resp_q.shape[1]
    group = resp_q.shape[2] // DH // kv
    store_rows = pool_dev * page_rows
    group_rows = mp * store_rows
    slots = dp * page_rows

    vmem = pl.BlockSpec(memory_space=pltpu.VMEM)
    smem = pl.BlockSpec(memory_space=pltpu.SMEM)
    hbm = pl.BlockSpec(memory_space=pl.ANY)
    dma = pltpu.SemaphoreType.DMA
    total = prompt_len + resp_len
    out_shape = (
        jax.ShapeDtypeStruct(resp_q.shape, BF16),
        jax.ShapeDtypeStruct(resp_kv.shape, BF16),
        jax.ShapeDtypeStruct(pool_pages.shape, F32),
    )
    buffers = [
        (pool_pages.shape, BF16),
        (resp_q.shape[1:], BF16),
        (d_out.shape[1:], BF16),
        (resp_kv.shape, BF16),
        (resp_q.shape[1:], BF16),
        (resp_kv.shape, BF16),
        (pool_pages.shape, F32),
        ((slots, group_rows), BF16),
        ((group_rows, slots), BF16),
        ((prompt_len, slots), BF16),
        ((slots, prompt_len), BF16),
        ((mp * chunks, store_rows, DH), BF16),
        ((chunks, group_rows, DH), BF16),
        ((chunks, slots, DH), BF16),
        ((chunks, slots, DH), BF16),
        ((chunks, slots, DH), BF16),
        ((chunks, slots, DH), BF16),
        ((group_rows, DH), F32),
        ((mp * chunks, store_rows, DH), BF16),
        ((chunks, mp, store_rows, DH), BF16),
        ((kv, group * resp_len, DH), BF16),
        ((kv, group * resp_len, DH), BF16),
        ((total, group * resp_len), F32),
        ((total, group * resp_len), F32),
        ((total, group * resp_len), BF16),
        ((total, group * resp_len), BF16),
    ]
    results = pl.pallas_call(
        functools.partial(kernel, dp, mp, kv, group),
        out_shape=out_shape,
        in_specs=[vmem] + [smem] * 3 + [pl.BlockSpec(memory_space=pltpu.HBM)] * 4,
        out_specs=(hbm, hbm, hbm),
        scratch_shapes=[pltpu.VMEM(shape, kind) for shape, kind in buffers]
        + [pltpu.SMEM((dp,), jnp.int32), dma((4,)), dma((3,))]
        + [dma((chunks,))] * 8,
        compiler_params=pltpu.CompilerParams(
            collective_id=0,
            has_side_effects=True,
            vmem_limit_bytes=56 << 20,
        ),
        cost_estimate=pl.CostEstimate(
            flops=10 * group * kv * resp_len * total * DH,
            bytes_accessed=8 * resp_q.shape[1] * resp_q.shape[2],
            transcendentals=group * kv * resp_len * total,
        ),
    )(
        pool_scales,
        fork,
        page_table.T,
        lengths,
        pool_pages,
        resp_q,
        d_out,
        resp_kv,
    )
    d_query, d_kv, d_pool = pl.pallas_call(
        settle,
        out_shape=out_shape,
        in_specs=[hbm] * 3,
        out_specs=(hbm, hbm, hbm),
        scratch_shapes=[pltpu.VMEM(o.shape, o.dtype) for o in out_shape] + [dma((2, 9))],
        compiler_params=pltpu.CompilerParams(vmem_limit_bytes=56 << 20),
    )(*results)
    return (d_query, d_kv, d_pool)


def solution(mesh):
    return jax.shard_map(
        per_device,
        mesh=mesh,
        in_specs=(
            P("dp", None, "mp"),
            P(None, "dp", None, "mp"),
            P("dp", None, "mp"),
            P("dp"),
            P(),
            P(),
            P(("dp", "mp"), None, None, None),
            P(("dp", "mp"), None, None),
        ),
        out_specs=(
            P("dp", None, "mp"),
            P(None, "dp", None, "mp"),
            P(("dp", "mp"), None, None, None),
        ),
        check_vma=False,
    )
```

```python
import functools
import math

import jax
import jax.numpy as jnp
from jax import lax
from jax.experimental import pallas as pl
from jax.experimental.pallas import tpu as pltpu
from jax.sharding import PartitionSpec as P

DH = 128
WIDTH = 1
MESH = pl.DeviceIdType.MESH
BF16 = jnp.bfloat16
F32 = jnp.float32
ACROSS = (((1,), (1,)), ((), ()))


def split_rows(rows):
    size = min(rows, 512)
    while rows % size:
        size //= 2
    return size, rows // size


def over_blocks(rows, body):
    size, count = split_rows(rows)
    if count == 1:
        body(0, size)
    else:

        @pl.loop(0, count)
        def _(b):
            body(pl.multiple_of(b * size, size), size)


def partner_order(count):
    half, quarter = count // 2, count // 4
    order = []
    for i in range(quarter):
        order += [half + i, half + quarter + i, quarter + i]
    rest = [k for k in range(1, count) if k not in order]
    return [k for k in order if 0 < k < count] + rest


def ones_where(hit):
    return jnp.where(hit, 1.0, 0.0).astype(BF16)


def kernel(
    dp,
    mp,
    kv,
    group,
    width,
    scales_ref,
    fork_ref,
    table_ref,
    length_ref,
    pages_hbm,
    q_hbm,
    g_hbm,
    rkv_hbm,
    dq_hbm,
    dkv_hbm,
    pool_hbm,
    pages_ref,
    q_buf,
    g_buf,
    rkv_buf,
    dq_buf,
    dkv_buf,
    pool_buf,
    pick,
    pick_t,
    take,
    take_t,
    slab,
    grouped,
    outgoing,
    arrived,
    back,
    returned,
    part_out,
    part_in,
    queries,
    grads,
    scores,
    grad_weights,
    weights_b,
    grad_scores,
    codes,
    in_sem,
    out_sem,
    mp_send,
    mp_recv,
    dp_send,
    dp_recv,
    rt_send,
    rt_recv,
    fm_send,
    fm_recv,
):
    my_dp = lax.axis_index("dp")
    my_mp = lax.axis_index("mp")
    pool_dev = scales_ref.shape[0]
    store_rows = pages_ref.shape[0]
    slot = store_rows // pool_dev
    page_rows = slot // 2
    group_pages = mp * pool_dev
    pages_prompt = table_ref.shape[0]
    resp_len = q_buf.shape[0]
    prompt_len = pages_prompt * page_rows
    total = prompt_len + resp_len
    chunks = kv // width
    span = width * DH
    inv_root = 1.0 / DH**0.5
    to_exp2 = inv_root * math.log2(math.e)

    pages_load = pltpu.make_async_copy(pages_hbm, pages_ref, in_sem.at[3])
    pages_load.start()
    barrier = pltpu.get_barrier_semaphore()

    @pl.loop(1, dp)
    def _(k):
        pl.semaphore_signal(
            barrier, inc=1, device_id={"dp": lax.rem(my_dp + k, dp)}, device_id_type=MESH
        )

    for k in range(1, mp):
        pl.semaphore_signal(
            barrier, inc=1, device_id={"mp": lax.rem(my_mp + k, mp)}, device_id_type=MESH
        )

    loads = [
        pltpu.make_async_copy(rkv_hbm, rkv_buf, in_sem.at[0]),
        pltpu.make_async_copy(q_hbm.at[0], q_buf, in_sem.at[1]),
        pltpu.make_async_copy(g_hbm.at[0], g_buf, in_sem.at[2]),
    ]
    for load in loads:
        load.start()

    iota = functools.partial(lax.broadcasted_iota, jnp.int32)
    ahead = iota((slot, pick.shape[1]), 1) - iota((slot, pick.shape[1]), 0)

    @pl.loop(0, dp, unroll=4 if dp % 4 == 0 else 1)
    def _(r):
        prompt_id = fork_ref[r]
        code = jnp.int32(-(1 << 20))
        for i in range(pages_prompt):
            page = table_ref[i, prompt_id]
            code = jnp.where(
                lax.div(page, group_pages) == my_dp, lax.rem(page, group_pages) * slot, code
            )
        codes[r] = code
        pick[pl.ds(pl.multiple_of(r * slot, slot), slot), :] = ones_where(ahead == code)

    factors = []
    for n in range(pool_dev):
        pair = scales_ref[n].astype(F32)
        for c in range(2):
            factors.append(jnp.broadcast_to(pair[c : c + 1, :], (page_rows, mp * kv)))
    factors = jnp.concatenate(factors, 0)
    my_rows = pl.ds(pl.multiple_of(my_mp * store_rows, store_rows), store_rows)
    pages_load.wait()
    for c in range(chunks):
        for m in range(mp):
            for i in range(width):
                head = m * kv + c * width + i
                scaled = (
                    pages_ref[:, head * DH : (head + 1) * DH].astype(F32)
                    * factors[:, head : head + 1]
                )
                slab[m * chunks + c, :, i * DH : (i + 1) * DH] = scaled.astype(BF16)
        if c == 0:
            pl.semaphore_wait(barrier, dp + mp - 2)
        for k in range(1, mp):
            other = lax.rem(my_mp + k, mp)
            pltpu.make_async_remote_copy(
                src_ref=slab.at[other * chunks + c],
                dst_ref=grouped.at[c, my_rows],
                send_sem=mp_send.at[c],
                recv_sem=mp_recv.at[c],
                device_id={"mp": other},
                device_id_type=MESH,
            ).start()
        grouped[c, my_rows] = slab[my_mp * chunks + c]

    def select(out_ref, matrix, operand):
        def body(start, size):
            rows = pl.ds(start, size)
            out_ref[rows, :] = jnp.dot(
                matrix[rows, :], operand, preferred_element_type=F32
            ).astype(out_ref.dtype)

        over_blocks(out_ref.shape[0], body)

    my_slot = pl.ds(pl.multiple_of(my_dp * slot, slot), slot)

    def exchange(c, source, target, send_sem, recv_sem):
        for k in partner_order(dp):
            other = lax.rem(my_dp + k, dp)
            pltpu.make_async_remote_copy(
                src_ref=source.at[c, pl.ds(pl.multiple_of(other * slot, slot), slot)],
                dst_ref=target.at[c, my_slot],
                send_sem=send_sem.at[c],
                recv_sem=recv_sem.at[c],
                device_id={"dp": other},
                device_id_type=MESH,
            ).start()
        target[c, my_slot] = source[c, my_slot]

    def wait_bytes(view, sem):
        pltpu.make_async_copy(view, view, sem).wait()

    dp_rows = pl.ds(0, (dp - 1) * slot)
    mp_rows = pl.ds(0, (mp - 1) * store_rows)
    for c in range(chunks):
        if mp > 1:
            wait_bytes(grouped.at[c, mp_rows], mp_recv.at[c])
        select(outgoing.at[c], pick, grouped[c])
        exchange(c, outgoing, arrived, dp_send, dp_recv)

    my_prompt = fork_ref[my_dp]
    sources = [
        lax.div(table_ref[i, my_prompt], group_pages) * slot for i in range(pages_prompt)
    ]
    ahead = iota((page_rows, dp * slot), 1) - iota((page_rows, dp * slot), 0)
    for c in range(2):
        for i in range(pages_prompt):
            take[pl.ds(c * prompt_len + i * page_rows, page_rows), :] = ones_where(
                ahead == sources[i] + c * page_rows
            )

    lane = iota((1, DH), 1)

    def transposed(out_ref, block, starts, piece):
        wanted = jnp.zeros((1, DH), jnp.int32)
        for i, start in enumerate(starts):
            wanted = jnp.where(lax.div(lane, piece) == i, start, wanted)
        wanted = wanted + lax.rem(lane, piece)

        def body(start, size):
            down = iota((size, DH), 0) + start
            out_ref[pl.ds(start, size), block * DH : (block + 1) * DH] = ones_where(down == wanted)

        over_blocks(out_ref.shape[0], body)

    per_block = DH // page_rows
    for block in range(2 * prompt_len // DH):
        pieces = [divmod(block * per_block + i, pages_prompt) for i in range(per_block)]
        starts = [sources[i] + c * page_rows for c, i in pieces]
        transposed(take_t, block, starts, page_rows)
    per_block = DH // slot
    for block in range(dp * slot // DH):
        starts = [codes[block * per_block + i] for i in range(per_block)]
        transposed(pick_t, block, starts, slot)
    for load in loads:
        load.wait()

    live = iota((resp_len, DH), 0) < length_ref[0]
    for h in range(kv * group):
        lanes = slice(h * DH, (h + 1) * DH)
        rows = pl.ds(h % group * resp_len, resp_len)
        queries[h // group, rows, :] = q_buf[:, lanes]
        grads[h // group, rows, :] = jnp.where(live, g_buf[:, lanes], jnp.zeros((), BF16))
    causal = iota((resp_len, resp_len), 0) <= iota((resp_len, resp_len), 1)

    def attend(j, prompt):
        lanes = slice(j * DH, (j + 1) * DH)
        keys = jnp.concatenate([prompt[:prompt_len], rkv_buf[0, 0, :, lanes]], 0)
        values = jnp.concatenate([prompt[prompt_len:], rkv_buf[1, 0, :, lanes]], 0)
        keys_t = keys.astype(F32).T.astype(BF16)
        scores[...] = lax.dot_general(keys, queries[j], ACROSS, preferred_element_type=F32)
        grad_weights[...] = lax.dot_general(
            values, grads[j], ACROSS, preferred_element_type=F32
        )
        for i in range(group):
            across = slice(i * resp_len, (i + 1) * resp_len)
            block = jnp.concatenate(
                [
                    scores[:prompt_len, across],
                    jnp.where(causal, scores[prompt_len:, across], -1e30),
                ],
                0,
            )
            top = jnp.max(block, axis=0, keepdims=True)
            powers = jnp.exp2((block - top) * to_exp2)
            weights = powers * (1.0 / jnp.sum(powers, axis=0, keepdims=True))
            rounded = weights.astype(BF16)
            change = grad_weights[:, across]
            delta = jnp.sum(rounded.astype(F32) * change, axis=0, keepdims=True)
            weights_b[:, across] = rounded
            grad_scores[:, across] = (weights * (change - delta)).astype(BF16)
        query_t = jnp.dot(keys_t, grad_scores[...], preferred_element_type=F32) * inv_root
        for i in range(group):
            h = j * group + i
            dq_buf[:, h * DH : (h + 1) * DH] = query_t[
                :, i * resp_len : (i + 1) * resp_len
            ].T.astype(BF16)
        key_grad = (
            jnp.dot(grad_scores[...], queries[j], preferred_element_type=F32) * inv_root
        )
        value_grad = jnp.dot(weights_b[...], grads[j], preferred_element_type=F32)
        dkv_buf[0, 0, :, lanes] = key_grad[prompt_len:].astype(BF16)
        dkv_buf[1, 0, :, lanes] = value_grad[prompt_len:].astype(BF16)
        prompt_grad = jnp.concatenate([key_grad[:prompt_len], value_grad[:prompt_len]], 0)
        return prompt_grad.astype(BF16)

    for c in range(chunks):
        wait_bytes(arrived.at[c, dp_rows], dp_recv.at[c])
        prompt = jnp.dot(take[...], arrived[c], preferred_element_type=F32).astype(BF16)
        parts = [
            attend(c * width + i, prompt[:, i * DH : (i + 1) * DH]) for i in range(width)
        ]
        prompt_grad = jnp.concatenate(parts, 1) if width > 1 else parts[0]
        select(back.at[c], take_t, prompt_grad)
        exchange(c, back, returned, rt_send, rt_recv)

    stores = [
        pltpu.make_async_copy(dq_buf, dq_hbm.at[0], out_sem.at[0]),
        pltpu.make_async_copy(dkv_buf, dkv_hbm, out_sem.at[1]),
    ]
    for store in stores:
        store.start()

    def column(m, c):
        return pl.ds(pl.multiple_of((m * chunks + c) * span, span), span)

    def settled(m, c, block):
        at = (slice(None), column(m, c))
        pool_buf[at] = block
        pltpu.make_async_copy(pool_buf.at[at], pool_hbm.at[at], out_sem.at[2]).start()

    def finish(c):
        if mp > 1:
            wait_bytes(part_in.at[c, pl.ds(0, mp - 1)], fm_recv.at[c])
        for k in range(1, mp):
            other = lax.rem(my_mp + k, mp)
            settled(other, c, part_in[c, other].astype(F32))

    def summed(m, c):
        rows = pl.ds(pl.multiple_of(m * store_rows, store_rows), store_rows)
        return jnp.dot(pick_t[rows, :], returned[c], preferred_element_type=F32)

    for c in range(chunks):
        wait_bytes(returned.at[c, dp_rows], rt_recv.at[c])
        for k in range(1, mp):
            other = lax.rem(my_mp + k, mp)
            part_out[other * chunks + c] = summed(other, c).astype(BF16)
            pltpu.make_async_remote_copy(
                src_ref=part_out.at[other * chunks + c],
                dst_ref=part_in.at[c, my_mp],
                send_sem=fm_send.at[c],
                recv_sem=fm_recv.at[c],
                device_id={"mp": other},
                device_id_type=MESH,
            ).start()
        settled(my_mp, c, summed(my_mp, c))
        if c > 0:
            finish(c - 1)
    finish(chunks - 1)
    for c in range(chunks):
        if mp > 1:
            wait_bytes(grouped.at[c, mp_rows], mp_send.at[c])
            wait_bytes(part_in.at[c, pl.ds(0, mp - 1)], fm_send.at[c])
        wait_bytes(arrived.at[c, dp_rows], dp_send.at[c])
        wait_bytes(returned.at[c, dp_rows], rt_send.at[c])
    for store in stores:
        store.wait()
    pltpu.make_async_copy(pool_buf, pool_hbm, out_sem.at[2]).wait()


def settle(dq_in, dkv_in, pool_in, dq_out, dkv_out, pool_out, dq_buf, dkv_buf, pool_buf, sem):
    pieces = []
    rows = dq_in.shape[1] // 4
    for i in range(4):
        at = (slice(None), pl.ds(i * rows, rows))
        pieces.append((dq_in.at[at], dq_buf.at[at], dq_out.at[at]))
    rows = pool_in.shape[0] // 4
    for i in range(4):
        at = pl.ds(i * rows, rows)
        pieces.append((pool_in.at[at], pool_buf.at[at], pool_out.at[at]))
    pieces.append((dkv_in, dkv_buf, dkv_out))
    reads, writes = [], []
    for i, (source, middle, target) in enumerate(pieces):
        reads.append(pltpu.make_async_copy(source, middle, sem.at[0, i]))
        writes.append(pltpu.make_async_copy(middle, target, sem.at[1, i]))
    for read in reads:
        read.start()
    for read, write in zip(reads, writes):
        read.wait()
        write.start()
    for write in writes:
        write.wait()


def per_device(resp_q, resp_kv, d_out, lengths, fork, page_table, pool_pages, pool_scales):
    dp = lax.axis_size("dp")
    mp = lax.axis_size("mp")
    pool_dev, _, page_rows, pool_width = pool_pages.shape
    heads_kv = pool_scales.shape[-1]
    kv = heads_kv // mp
    width = WIDTH if kv % WIDTH == 0 else 1
    chunks, span = kv // width, width * DH
    pages_prompt = page_table.shape[1]
    prompt_len = pages_prompt * page_rows
    resp_len = resp_q.shape[1]
    group = resp_q.shape[2] // DH // kv
    slot = 2 * page_rows
    store_rows = pool_dev * slot
    group_rows = mp * store_rows
    slots = dp * slot

    vmem = pl.BlockSpec(memory_space=pltpu.VMEM)
    smem = pl.BlockSpec(memory_space=pltpu.SMEM)
    hbm = pl.BlockSpec(memory_space=pl.ANY)
    dma = pltpu.SemaphoreType.DMA
    total = prompt_len + resp_len
    out_shape = (
        jax.ShapeDtypeStruct(resp_q.shape, BF16),
        jax.ShapeDtypeStruct(resp_kv.shape, BF16),
        jax.ShapeDtypeStruct((store_rows, pool_width), F32),
    )
    buffers = [
        ((store_rows, pool_width), BF16),
        (resp_q.shape[1:], BF16),
        (d_out.shape[1:], BF16),
        (resp_kv.shape, BF16),
        (resp_q.shape[1:], BF16),
        (resp_kv.shape, BF16),
        ((store_rows, pool_width), F32),
        ((slots, group_rows), BF16),
        ((group_rows, slots), BF16),
        ((2 * prompt_len, slots), BF16),
        ((slots, 2 * prompt_len), BF16),
        ((mp * chunks, store_rows, span), BF16),
        ((chunks, group_rows, span), BF16),
        ((chunks, slots, span), BF16),
        ((chunks, slots, span), BF16),
        ((chunks, slots, span), BF16),
        ((chunks, slots, span), BF16),
        ((mp * chunks, store_rows, span), BF16),
        ((chunks, mp, store_rows, span), BF16),
        ((kv, group * resp_len, DH), BF16),
        ((kv, group * resp_len, DH), BF16),
        ((total, group * resp_len), F32),
        ((total, group * resp_len), F32),
        ((total, group * resp_len), BF16),
        ((total, group * resp_len), BF16),
    ]
    results = pl.pallas_call(
        functools.partial(kernel, dp, mp, kv, group, width),
        out_shape=out_shape,
        in_specs=[vmem] + [smem] * 3 + [pl.BlockSpec(memory_space=pltpu.HBM)] * 4,
        out_specs=(hbm, hbm, hbm),
        scratch_shapes=[pltpu.VMEM(shape, kind) for shape, kind in buffers]
        + [pltpu.SMEM((dp,), jnp.int32), dma((4,)), dma((3,))]
        + [dma((chunks,))] * 8,
        compiler_params=pltpu.CompilerParams(
            collective_id=0,
            has_side_effects=True,
            vmem_limit_bytes=56 << 20,
        ),
        cost_estimate=pl.CostEstimate(
            flops=10 * group * kv * resp_len * total * DH,
            bytes_accessed=8 * resp_q.shape[1] * resp_q.shape[2],
            transcendentals=group * kv * resp_len * total,
        ),
    )(
        pool_scales,
        fork,
        page_table.T,
        lengths,
        pool_pages.reshape(store_rows, pool_width),
        resp_q,
        d_out,
        resp_kv,
    )
    d_query, d_kv, d_pool = pl.pallas_call(
        settle,
        out_shape=out_shape,
        in_specs=[hbm] * 3,
        out_specs=(hbm, hbm, hbm),
        scratch_shapes=[pltpu.VMEM(o.shape, o.dtype) for o in out_shape] + [dma((2, 9))],
        compiler_params=pltpu.CompilerParams(vmem_limit_bytes=56 << 20),
    )(*results)
    return (d_query, d_kv, d_pool.reshape(pool_pages.shape))


def solution(mesh):
    return jax.shard_map(
        per_device,
        mesh=mesh,
        in_specs=(
            P("dp", None, "mp"),
            P(None, "dp", None, "mp"),
            P("dp", None, "mp"),
            P("dp"),
            P(),
            P(),
            P(("dp", "mp"), None, None, None),
            P(("dp", "mp"), None, None),
        ),
        out_specs=(
            P("dp", None, "mp"),
            P(None, "dp", None, "mp"),
            P(("dp", "mp"), None, None, None),
        ),
        check_vma=False,
    )
```
